32 devices in a mesh: grp: 2 (over y), wide: 8 (over z, core), pair: 2 (over x).
Axes of the slice: x: 2, y: 2, z: 4, core: 2. Of those that a mesh axis runs over, the one named last changes fastest.
Arguments:
- amplitudes: bfloat16 [2048, 3584], P(('grp', 'wide', 'pair')), parts along dimension 0, may hold values from -6 to 6
- integrals: bfloat16 [7168, 3584], P(('grp', 'wide'), 'pair'), parts along dimension 0, may hold values from -0.1875 to 0.1875
- tile_list: int32 [32, 28], P('grp'), parts along dimension 0, may hold values from 0 to 55, all different within a row
- slab_order: int32 [32], P('grp'), parts along dimension 0, may hold values from 0 to 15, each once
- block_list: int32 [112, 2, 14], P('grp'), parts along dimension 0, may hold values from 0 to 27, all different within a row
Outputs:
- ladder: float32 [2048, 3584], P(('grp', 'wide', 'pair')), parts along dimension 0
The draws below stay inside these ranges and needn't reach their ends.
There are 2 independent parts, one for each index of `grp`. The reference program is written for one: setup_inputs(seed, part) draws one part's arguments, and reference() takes and returns one part's arrays. A program takes and returns all parts, laid end to end along the dimension named above; each array names one. Nothing has to cross between parts.
Inputs may be any that keep to these rules, and one draw needn't show every extreme that they name: `tile_list`: each row names 28 different tiles, and every tile is named by some row. `slab_order`: each tile position holds a different occupied-pair tile. `block_list`: each last-dimension row names 14 different tiles of its group.
All inputs are finite; a program needn't handle non-finite values.
Results may differ from the reference program's by a relative error of at most 0.0003.
Values may be sent and summed in bfloat16 or wider, within the bound.
No kernel may reach another device: no remote copies, remote signals or barrier semaphores. Data moves between devices by JAX's collectives and lax.ppermute only.
A program may use at most 192 MiB of HBM per device.

```python
import jax
import jax.numpy as jnp
from jax import lax

BLK = 64
VT = 56
VP = 3584
OB = 16
OP = 1024
KEEP = 28
PGRP = 28
KEEPV = 14
N_PAIR = 2


def block_levels(stream_key, dims, split, smallest, high):
    level, own = 1.0, jax.random.fold_in(stream_key, 6)
    for position, parts in split:
        steps = jnp.exp(jax.random.uniform(jax.random.fold_in(own, position), (parts,), jnp.float32, smallest / len(split), high / len(split)))
        level = level * jnp.repeat(steps, dims[position] // parts).reshape([-1 if axis == position else 1 for axis in range(len(dims))])
    return level


def choose_distinct(rng, rows, amount, top, lift):
    order = jax.random.permutation(jax.random.fold_in(rng, 1), amount)
    pull = order
    for power in range(3):
        pull = pull * pull // amount
    pull = pull * lift // amount
    chance = jax.random.randint(jax.random.fold_in(rng, 2), (rows, amount), 0, 4096) + pull
    fixed_rows = jax.random.permutation(jax.random.fold_in(rng, 3), rows)[jnp.arange(amount) % rows]
    chance = jnp.where(jnp.arange(rows)[:, None] == fixed_rows[None, :], 1 << 14, chance)
    score = chance * amount + jnp.arange(amount)
    return lax.top_k(score.astype(jnp.int32), top)[1].astype(jnp.int32)


def centred(key, dims, scale, reach, shards=(), held_as=jnp.bfloat16):
    loudness = block_levels(key, dims, shards, -0.22, 0.18) if shards else 1.0
    array = jax.random.normal(key, dims, jnp.float32) * scale * loudness
    return jnp.minimum(jnp.maximum(array, -reach), reach).astype(held_as)


def setup_inputs(seed: int = 0, part: int = 0) -> dict:
    seeds = jax.random.split(jax.random.key(seed), 6)
    own_keys = jax.random.split(jax.random.fold_in(seeds[5], part), 6)
    return {
        "amplitudes": centred(own_keys[0], (OP, VP), 1.0, 6.0, ((0, 16),)),
        "integrals": centred(own_keys[1], (VP, VP), (VP // 4) ** -0.5, 0.1875, ((0, 8), (1, 2))),
        "tile_list": choose_distinct(own_keys[2], OB, VT, KEEP, 8192),
        "slab_order": jax.random.permutation(own_keys[3], OB).astype(jnp.int32),
        "block_list": choose_distinct(own_keys[4], VT * N_PAIR, PGRP, KEEPV, 4096).reshape((VT, N_PAIR, KEEPV)),
    }


def reference(amplitudes, integrals, tile_list, slab_order, block_list):
    listed = jnp.take(tile_list, slab_order, axis=0)
    tile_ids = jnp.arange(VT, dtype=jnp.int32)
    present = jnp.any(listed[:, :, None] == tile_ids[None, None, :], axis=1).astype(jnp.float32)
    masked_amplitudes = amplitudes.astype(jnp.float32).reshape(OB, BLK, VT, BLK) * present[:, None, :, None]
    masked_amplitudes = masked_amplitudes.reshape(OP, VP)
    group_ids = jnp.arange(PGRP, dtype=jnp.int32)
    live = jnp.any(block_list[:, :, :, None] == group_ids[None, None, None, :], axis=2)
    live = live.reshape(VT, VT).astype(jnp.float32)
    masked_integrals = integrals.astype(jnp.float32).reshape(VT, BLK, VT, BLK) * live[:, None, :, None]
    masked_integrals = masked_integrals.reshape(VP, VP)
    return jnp.dot(masked_amplitudes, masked_integrals, precision=lax.Precision.HIGHEST, preferred_element_type=jnp.float32)
```

```python
import functools

import jax
import jax.numpy as jnp
from jax import lax
from jax.experimental import pallas as pl
from jax.experimental.pallas import tpu as pltpu
from jax.sharding import PartitionSpec as P

BLK = 64
LANES = 128
GROUP = 256
LOW_EXP = -100.0
VMEM = pl.BlockSpec(memory_space=pltpu.VMEM)
SMEM = pl.BlockSpec(memory_space=pltpu.SMEM)
PARAMS = pltpu.CompilerParams(vmem_limit_bytes=48 * 1024 * 1024)


def gather_body(amplitudes, integrals, tile_list, slab_order, block_list):
    rows_dev, virt_cols = amplitudes.shape
    virt_tiles = virt_cols // BLK
    own_count = rows_dev // BLK
    pair_count = lax.axis_size("pair")
    group_count = own_count * pair_count
    wide_index = lax.axis_index("wide")
    pair_index = lax.axis_index("pair")
    slab_ids = lax.dynamic_slice_in_dim(slab_order, wide_index * group_count, group_count)
    own_ids = lax.dynamic_slice_in_dim(slab_ids, pair_index * own_count, own_count)
    own_lists = jnp.take(tile_list, own_ids, axis=0)
    tiles_four = amplitudes.reshape(own_count, BLK, virt_tiles, BLK)
    tile_ids = jnp.arange(virt_tiles, dtype=jnp.int32)
    present = jnp.any(own_lists[:, :, None] == tile_ids[None, None, :], axis=1).astype(
        amplitudes.dtype
    )
    masked = (tiles_four * present[:, None, :, None]).reshape(rows_dev, virt_cols)
    slab_rows = lax.all_gather(masked, "pair", axis=0, tiled=True)
    group_tiles = integrals.shape[1] // BLK
    my_lists = lax.dynamic_index_in_dim(block_list, pair_index, 1, keepdims=False)
    group_ids = jnp.arange(group_tiles, dtype=jnp.int32)
    live = jnp.any(my_lists[:, :, None] == group_ids[None, None, :], axis=1).astype(integrals.dtype)
    shard_block = lax.all_gather(integrals, "wide", axis=0, tiled=True)
    qtiles = shard_block.shape[0] // BLK
    masked_block = shard_block.reshape(qtiles, BLK, group_tiles, BLK) * live[:, None, :, None]
    masked_block = masked_block.reshape(shard_block.shape)
    ladder_slab = jnp.dot(slab_rows, masked_block, preferred_element_type=jnp.float32)
    return lax.all_to_all(ladder_slab, "pair", split_axis=0, concat_axis=1, tiled=True)


def low_lanes(rows):
    return lax.broadcasted_iota(jnp.int32, (rows, LANES), 1) < BLK


def half(index):
    return pl.ds(pl.multiple_of((index // 2) * LANES, LANES), LANES)


def pack_kernel(lists, block_ref, first_ref, second_ref):
    wide, pair = lax.axis_index("wide"), lax.axis_index("pair")
    tiles = block_ref.shape[0] // BLK
    keep = first_ref.shape[1] // BLK
    split = first_ref.shape[0] // BLK
    low = low_lanes(BLK)
    for i in range(tiles):
        out, row = (first_ref, i) if i < split else (second_ref, i - split)
        base = ((wide * tiles + i) * 2 + pair) * keep
        rows = pl.ds(i * BLK, BLK)
        for j in range(keep // 2):
            even, odd = lists[base + 2 * j], lists[base + 2 * j + 1]
            left = pltpu.roll(block_ref[rows, half(even)], (even % 2) * BLK, 1)
            right = pltpu.roll(block_ref[rows, half(odd)], BLK - (odd % 2) * BLK, 1)
            out[row * BLK : (row + 1) * BLK, j * LANES : (j + 1) * LANES] = jnp.where(
                low, left, right
            )


def mask_kernel(tile_list, slab_order, amp_ref, own_ref, far_ref, present, masked):
    wide, pair = lax.axis_index("wide"), lax.axis_index("pair")
    count = amp_ref.shape[1] // BLK
    keep = tile_list.shape[1]
    tile = slab_order[wide * 2 + pair]
    for t in range(count):
        present[t] = 0
    for k in range(keep):
        present[tile_list[tile, k]] = 1
    low = lax.broadcasted_iota(jnp.int32, (BLK, LANES), 1) < BLK
    for s in range(count // 2):
        cols = slice(s * LANES, (s + 1) * LANES)
        flag = jnp.where(low, present[2 * s], present[2 * s + 1])
        masked[:, cols] = jnp.where(flag > 0, amp_ref[:, cols], 0)
    mine = wide // 4
    part = amp_ref.shape[1] // 8
    room = own_ref.shape[1] // 4
    for side, out in ((mine, own_ref), (1 - mine, far_ref)):
        rows = masked[:, pl.ds(pl.multiple_of(side * 4 * part, LANES), 4 * part)]
        for w in range(4):
            out[:, w * room : w * room + part] = rows[:, w * part : (w + 1) * part]
            out[:, w * room + part : (w + 1) * room] = jnp.zeros((BLK, room - part), out.dtype)


def gather_rows(amps, rows_ref, source, offset, depth, room):
    cols = pl.ds(pl.multiple_of(source * room + offset, LANES), depth)
    for n, amp in enumerate(amps):
        rows_ref[n * BLK : (n + 1) * BLK, 0:depth] = amp[:, cols]


def raw_kernel(place, own_ref, near_ref, a0, a1, a2, a3, acc_ref, dense, rows):
    wide = lax.axis_index("wide")
    tiles = own_ref.shape[0] // BLK
    group = own_ref.shape[1] // BLK
    depth = own_ref.shape[0]
    room = a0.shape[1] // 4
    low = low_lanes(BLK)
    for n, (block, source) in enumerate(((own_ref, wide), (near_ref, wide ^ 1))):
        for i in range(tiles):
            here = slice(i * BLK, (i + 1) * BLK)
            base = (source * tiles + i) * group
            for s in range(group // 2):
                cols = slice(s * LANES, (s + 1) * LANES)
                flag = jnp.where(low, place[base + 2 * s], place[base + 2 * s + 1])
                dense[here, cols] = jnp.where(flag >= 0, block[here, cols], 0)
        gather_rows((a0, a1, a2, a3), rows, source % 4, 0, depth, room)
        product = jnp.dot(rows[...], dense[...], preferred_element_type=jnp.float32)
        if n == 0:
            acc_ref[...] = product
        else:
            acc_ref[...] += product


def spread(place, packed, swapped, dense, source_row):
    tiles = packed.shape[0] // BLK
    keep = packed.shape[1] // BLK
    group = dense.shape[1] // BLK
    low = low_lanes(BLK)
    for j in range(keep // 2):
        cols = slice(j * LANES, (j + 1) * LANES)
        swapped[0, :, cols] = packed[:, cols]
        swapped[1, :, cols] = pltpu.roll(packed[:, cols], BLK, 1)
    for i in range(tiles):
        here = slice(i * BLK, (i + 1) * BLK)
        base = (source_row + i) * group
        for s in range(group // 2):
            even, odd = place[base + 2 * s], place[base + 2 * s + 1]
            left_at, right_at = jnp.maximum(even, 0), jnp.maximum(odd, 0)
            left = swapped[left_at % 2, here, half(left_at)]
            right = swapped[1 - right_at % 2, here, half(right_at)]
            flag = jnp.where(low, even, odd)
            dense[here, s * LANES : (s + 1) * LANES] = jnp.where(
                flag >= 0, jnp.where(low, left, right), 0
            )


def packed_product(place, blocks, amps, first_tile, swapped, dense, rows):
    wide = lax.axis_index("wide")
    depth = blocks[0].shape[0]
    room = amps[0].shape[1] // 4
    tiles = room // BLK - 1
    total = None
    for block, source in zip(blocks, (wide ^ 2, wide ^ 3)):
        spread(place, block, swapped, dense, source * tiles + first_tile)
        gather_rows(amps, rows, source % 4, first_tile * BLK, depth, room)
        product = jnp.dot(rows[...], dense[...], preferred_element_type=jnp.float32)
        total = product if total is None else total + product
    return total


def first_kernel(place, z_ref, y_ref, a0, a1, a2, a3, acc_ref, sum_ref, swapped, dense, rows):
    product = packed_product(place, (z_ref, y_ref), (a0, a1, a2, a3), 0, swapped, dense, rows)
    sum_ref[...] = acc_ref[...] + product


def encode(values, out):
    width = values.shape[1]
    lane = lax.broadcasted_iota(jnp.int32, (BLK, LANES), 1)
    exps = jnp.zeros((BLK, LANES), jnp.int32)
    for g in range(width // GROUP):
        part = values[:, g * GROUP : (g + 1) * GROUP]
        top = jnp.max(jnp.abs(part), axis=1, keepdims=True)
        exp = jnp.maximum(jnp.ceil(jnp.log2(jnp.maximum(top, 2.0**LOW_EXP))), LOW_EXP)
        scaled = jnp.clip(jnp.round(part * jnp.exp2(15.0 - exp)), -32767.0, 32767.0)
        out[:, g * GROUP : (g + 1) * GROUP] = scaled.astype(jnp.int32).astype(jnp.int16)
        exps = jnp.where(lane == g, exp.astype(jnp.int32), exps)
    out[:, width : width + LANES] = exps.astype(jnp.int16)


def last_kernel(
    place, z_ref, y_ref, a0, a1, a2, a3, acc_ref, keep_ref, send_ref, same_ref, cross_ref,
    swapped, dense, rows,
):
    first_tile = a0.shape[1] // 4 // BLK - 1 - z_ref.shape[0] // BLK
    product = packed_product(
        place, (z_ref, y_ref), (a0, a1, a2, a3), first_tile, swapped, dense, rows
    )
    total = acc_ref[...] + product
    keep_ref[...] = total[0 * BLK : 1 * BLK]
    send_ref[...] = total[1 * BLK : 2 * BLK]
    encode(total[2 * BLK : 3 * BLK], same_ref)
    encode(total[3 * BLK : 4 * BLK], cross_ref)


def join_kernel(keep_ref, got_ref, same_ref, cross_ref, out_ref):
    pair = lax.axis_index("pair")
    width = keep_ref.shape[1]
    for side, base, coded in ((pair, keep_ref, same_ref), (1 - pair, got_ref, cross_ref)):
        exps = coded[:, width : width + LANES].astype(jnp.int32).astype(jnp.float32)
        for g in range(width // GROUP):
            cols = slice(g * GROUP, (g + 1) * GROUP)
            scale = jnp.exp2(exps[:, g : g + 1] - 15.0)
            value = coded[:, cols].astype(jnp.int32).astype(jnp.float32) * scale
            where = pl.ds(pl.multiple_of(side * width + g * GROUP, LANES), GROUP)
            out_ref[:, where] = base[:, cols] + value


def call(kernel, out, operands, smem, scratch=(), flops=0):
    moved = sum(a.size * a.dtype.itemsize for a in operands)
    return pl.pallas_call(
        kernel,
        out_shape=out,
        in_specs=[SMEM] * smem + [VMEM] * (len(operands) - smem),
        out_specs=jax.tree.map(lambda _: VMEM, out),
        scratch_shapes=list(scratch),
        compiler_params=PARAMS,
        cost_estimate=pl.CostEstimate(flops=flops, bytes_accessed=moved, transcendentals=0),
    )(*operands)


def swap_body(amplitudes, integrals, tile_list, slab_order, block_list):
    wide_count, pair_count = lax.axis_size("wide"), lax.axis_size("pair")
    depth, width = integrals.shape
    tiles, group = depth // BLK, width // BLK
    keep = block_list.shape[2]
    bf16, f32, i16 = jnp.bfloat16, jnp.float32, jnp.int16
    sds = jax.ShapeDtypeStruct

    def move(x, flip_wide, flip_pair=0):
        if flip_wide and flip_pair:
            n = wide_count * pair_count
            flip = flip_wide * pair_count + flip_pair
            return lax.ppermute(x, ("wide", "pair"), [(i, i ^ flip) for i in range(n)])
        if flip_wide:
            return lax.ppermute(x, "wide", [(i, i ^ flip_wide) for i in range(wide_count)])
        return lax.ppermute(x, "pair", [(i, i ^ flip_pair) for i in range(pair_count)])

    split = (tiles + 1) // 2
    cut = split * BLK
    first, second = call(
        pack_kernel,
        (sds((cut, keep * BLK), bf16), sds((depth - cut, keep * BLK), bf16)),
        (block_list.reshape(-1), integrals),
        1,
    )
    room = depth + BLK
    own, far = call(
        mask_kernel,
        (sds((BLK, 4 * room), bf16),) * 2,
        (tile_list, slab_order, amplitudes),
        2,
        [pltpu.SMEM((amplitudes.shape[1] // BLK,), jnp.int32), pltpu.VMEM(amplitudes.shape, bf16)],
    )
    near = move(integrals, 1)
    z_first = move(first, 2)
    z_second = move(second, 2)
    far_same = move(far, 4)
    own_cross = move(own, 0, 1)
    far_cross = move(far_same, 0, 1)
    amps = (own, own_cross, far_same, far_cross)

    my_lists = lax.dynamic_index_in_dim(block_list, lax.axis_index("pair"), 1, keepdims=False)
    hit = my_lists[:, :, None] == jnp.arange(group, dtype=jnp.int32)[None, None, :]
    order = jnp.arange(1, keep + 1, dtype=jnp.int32)[None, :, None]
    place = (jnp.sum(jnp.where(hit, order, 0), axis=1) - 1).reshape(-1)

    rows = 4 * BLK
    acc = call(
        raw_kernel,
        sds((rows, width), f32),
        (place, integrals, near, *amps),
        1,
        [pltpu.VMEM((depth, width), bf16), pltpu.VMEM((rows, depth), bf16)],
        2 * 2 * rows * depth * width,
    )
    y_first = move(z_first, 1)
    y_second = move(z_second, 1)

    def scratch(n):
        return [
            pltpu.VMEM((2, n, keep * BLK), bf16),
            pltpu.VMEM((n, width), bf16),
            pltpu.VMEM((rows, n), bf16),
        ]

    acc = call(
        first_kernel,
        sds((rows, width), f32),
        (place, z_first, y_first, *amps, acc),
        1,
        scratch(cut),
        2 * 2 * rows * cut * width,
    )
    keep_rows, send_rows, same, cross = call(
        last_kernel,
        (sds((BLK, width), f32),) * 2 + (sds((BLK, width + LANES), i16),) * 2,
        (place, z_second, y_second, *amps, acc),
        1,
        scratch(depth - cut),
        2 * 2 * rows * (depth - cut) * width,
    )
    same = move(same, 4)
    cross = move(cross, 4, 1)
    got = move(send_rows, 0, 1)
    return call(
        join_kernel,
        sds((BLK, pair_count * width), f32),
        (keep_rows, got, same, cross),
        0,
    )


def solution(mesh):
    placed = (
        P(("grp", "wide", "pair"), None),
        P(("grp", "wide"), "pair"),
        P("grp", None),
        P("grp"),
        P("grp", None, None),
    )
    swapped = mesh.shape["wide"] == 8 and mesh.shape["pair"] == 2
    return jax.shard_map(
        swap_body if swapped else gather_body,
        mesh=mesh,
        in_specs=placed,
        out_specs=P(("grp", "wide", "pair"), None),
        check_vma=False,
    )
```

```python
import functools

import jax
import jax.numpy as jnp
from jax import lax
from jax.experimental import pallas as pl
from jax.experimental.pallas import tpu as pltpu
from jax.sharding import PartitionSpec as P

BLK = 64
LANES = 128
GROUP = 256
LOW_EXP = -100.0
ROOM = 60
SPLIT = 3
VMEM = pl.BlockSpec(memory_space=pltpu.VMEM)
SMEM = pl.BlockSpec(memory_space=pltpu.SMEM)
MIB = 1024 * 1024


def gather_body(amplitudes, integrals, tile_list, slab_order, block_list):
    rows_dev, virt_cols = amplitudes.shape
    virt_tiles = virt_cols // BLK
    own_count = rows_dev // BLK
    pair_count = lax.axis_size("pair")
    group_count = own_count * pair_count
    wide_index = lax.axis_index("wide")
    pair_index = lax.axis_index("pair")
    slab_ids = lax.dynamic_slice_in_dim(slab_order, wide_index * group_count, group_count)
    own_ids = lax.dynamic_slice_in_dim(slab_ids, pair_index * own_count, own_count)
    own_lists = jnp.take(tile_list, own_ids, axis=0)
    tiles_four = amplitudes.reshape(own_count, BLK, virt_tiles, BLK)
    tile_ids = jnp.arange(virt_tiles, dtype=jnp.int32)
    present = jnp.any(own_lists[:, :, None] == tile_ids[None, None, :], axis=1).astype(
        amplitudes.dtype
    )
    masked = (tiles_four * present[:, None, :, None]).reshape(rows_dev, virt_cols)
    slab_rows = lax.all_gather(masked, "pair", axis=0, tiled=True)
    group_tiles = integrals.shape[1] // BLK
    my_lists = lax.dynamic_index_in_dim(block_list, pair_index, 1, keepdims=False)
    group_ids = jnp.arange(group_tiles, dtype=jnp.int32)
    live = jnp.any(my_lists[:, :, None] == group_ids[None, None, :], axis=1).astype(integrals.dtype)
    shard_block = lax.all_gather(integrals, "wide", axis=0, tiled=True)
    qtiles = shard_block.shape[0] // BLK
    masked_block = shard_block.reshape(qtiles, BLK, group_tiles, BLK) * live[:, None, :, None]
    masked_block = masked_block.reshape(shard_block.shape)
    ladder_slab = jnp.dot(slab_rows, masked_block, preferred_element_type=jnp.float32)
    return lax.all_to_all(ladder_slab, "pair", split_axis=0, concat_axis=1, tiled=True)


def low_lanes(rows):
    return lax.broadcasted_iota(jnp.int32, (rows, LANES), 1) < BLK


def half(index):
    return pl.ds(pl.multiple_of((index // 2) * LANES, LANES), LANES)


def fetch(pairs, sems):
    copies = [pltpu.make_async_copy(s, d, sems.at[n]) for n, (s, d) in enumerate(pairs)]
    for copy in copies:
        copy.start()
    return copies


def pack_kernel(lists_ref, block_ref, first_ref, second_ref, lists, block, sems):
    wide, pair = lax.axis_index("wide"), lax.axis_index("pair")
    tiles = block_ref.shape[0] // BLK
    keep = first_ref.shape[1] // BLK
    split = first_ref.shape[0] // BLK
    rows = [pl.ds(i * BLK, BLK) for i in range(tiles)]
    copies = fetch([(lists_ref, lists)] + [(block_ref.at[r], block.at[r]) for r in rows], sems)
    copies[0].wait()
    low = low_lanes(BLK)
    for i in range(tiles):
        copies[1 + i].wait()
        out, row = (first_ref, i) if i < split else (second_ref, i - split)
        u = wide * tiles + i
        for j in range(keep // 2):
            even, odd = lists[2 * j, pair, u], lists[2 * j + 1, pair, u]
            left = pltpu.roll(block[rows[i], half(even)], (even % 2) * BLK, 1)
            right = pltpu.roll(block[rows[i], half(odd)], BLK - (odd % 2) * BLK, 1)
            out[row * BLK : (row + 1) * BLK, j * LANES : (j + 1) * LANES] = jnp.where(
                low, left, right
            )


def mask_kernel(tile_ref, slab_ref, amp_ref, own_ref, far_ref, tile_list, slab, amp, present, sems):
    wide, pair = lax.axis_index("wide"), lax.axis_index("pair")
    copies = fetch([(tile_ref, tile_list), (slab_ref, slab), (amp_ref, amp)], sems)
    count = amp_ref.shape[1] // BLK
    for t in range(count):
        present[t] = 0
    copies[0].wait()
    copies[1].wait()
    tile = slab[wide * 2 + pair]
    for k in range(tile_ref.shape[1]):
        present[tile_list[tile, k]] = 1
    copies[2].wait()
    mine = wide // 4
    low = low_lanes(BLK)
    blocks = count // 4
    for side, out in ((mine, own_ref), (1 - mine, far_ref)):
        for s in range(blocks):
            t = 2 * (side * blocks + s)
            flag = jnp.where(low, present[t], present[t + 1])
            out[:, s * LANES : (s + 1) * LANES] = jnp.where(flag > 0, amp[:, half(t)], 0)


def raw_kernel(place, own_ref, near_ref, dense):
    wide = lax.axis_index("wide")
    depth, width = own_ref.shape
    tiles, group = depth // BLK, width // BLK
    low = low_lanes(BLK)
    for block, source in ((own_ref, wide), (near_ref, wide ^ 1)):
        for i in range(tiles):
            base = (source * tiles + i) * group
            here = pl.ds(pl.multiple_of((source % 2) * depth + i * BLK, BLK), BLK)
            for s in range(group // 2):
                cols = slice(s * LANES, (s + 1) * LANES)
                flag = jnp.where(low, place[base + 2 * s], place[base + 2 * s + 1])
                dense[here, cols] = jnp.where(flag >= 0, block[i * BLK : (i + 1) * BLK, cols], 0)


def spread(place, packed, dense, source_row):
    tiles = packed.shape[0] // BLK
    group = dense.shape[1] // BLK
    low = low_lanes(BLK)
    for i in range(tiles):
        here = slice(i * BLK, (i + 1) * BLK)
        base = (source_row + i) * group
        for s in range(group // 2):
            even, odd = place[base + 2 * s], place[base + 2 * s + 1]
            left_at, right_at = jnp.maximum(even, 0), jnp.maximum(odd, 0)
            left = pltpu.roll(packed[here, half(left_at)], (left_at % 2) * BLK, 1)
            right = pltpu.roll(packed[here, half(right_at)], BLK - (right_at % 2) * BLK, 1)
            flag = jnp.where(low, even, odd)
            dense[here, s * LANES : (s + 1) * LANES] = jnp.where(
                flag >= 0, jnp.where(low, left, right), 0
            )


def pick(amps, rows, starts):
    count = rows.shape[1] // BLK // len(starts)
    low = low_lanes(BLK)
    for b in range(rows.shape[1] // LANES):
        even, odd = (starts[d // count] + d % count for d in (2 * b, 2 * b + 1))
        for n, amp in enumerate(amps):
            left = pltpu.roll(amp[:, half(even)], (even % 2) * BLK, 1)
            right = pltpu.roll(amp[:, half(odd)], BLK - (odd % 2) * BLK, 1)
            rows[n * BLK : (n + 1) * BLK, b * LANES : (b + 1) * LANES] = jnp.where(low, left, right)


def dot(a, b):
    return jnp.dot(a, b, preferred_element_type=jnp.float32)


def spread_kernel(tiles, first, place, z_ref, y_ref, dense):
    wide = lax.axis_index("wide")
    for n, (block, source) in enumerate(((z_ref, wide ^ 2), (y_ref, wide ^ 3))):
        rows = block.shape[0]
        spread(place, block, dense.at[n * rows : (n + 1) * rows], source * tiles + first)


def chip_rows(amps, rows):
    at = (lax.axis_index("wide") // 2) % 2
    depth = rows.shape[1]
    for n, amp in enumerate(amps):
        rows[n * BLK : (n + 1) * BLK] = amp[:, pl.ds(pl.multiple_of(at * depth, LANES), depth)]


def meet(amps, tiles, first, rows, dense):
    wide = lax.axis_index("wide")
    pick(amps, rows, [(source % 4) * tiles + first for source in (wide ^ 2, wide ^ 3)])
    return dot(rows[...], dense[...])


def early_kernel(tiles, raw, dense, a0, a1, a2, a3, acc_ref, raw_rows, rows):
    amps = (a0, a1, a2, a3)
    chip_rows(amps, raw_rows)
    acc_ref[...] = dot(raw_rows[...], raw[...]) + meet(amps, tiles, 0, rows, dense)


def encode(values, out):
    width = values.shape[1]
    across = width // LANES
    high = out.shape[1]
    groups = width // GROUP
    lane = lax.broadcasted_iota(jnp.int32, (high, LANES), 1)
    exps = jnp.zeros((high, LANES), jnp.int32)
    for i in range(BLK // high):
        for g in range(groups):
            part = values[i * high : (i + 1) * high, g * GROUP : (g + 1) * GROUP]
            top = jnp.max(jnp.abs(part), axis=1, keepdims=True)
            exp = jnp.maximum(jnp.ceil(jnp.log2(jnp.maximum(top, 2.0**LOW_EXP))), LOW_EXP)
            scaled = jnp.clip(jnp.round(part * jnp.exp2(15.0 - exp)), -32767.0, 32767.0)
            coded = scaled.astype(jnp.int32).astype(jnp.int16)
            for k in range(GROUP // LANES):
                at = i * across + g * (GROUP // LANES) + k
                out[at] = coded[:, k * LANES : (k + 1) * LANES]
            exps = jnp.where(lane == i * groups + g, exp.astype(jnp.int32), exps)
    out[out.shape[0] - 1] = exps.astype(jnp.int16)


def last_kernel(
    tiles, first, place, z_ref, y_ref, a0, a1, a2, a3, acc_ref, keep_ref, upper_ref, lower_ref,
    same_ref, cross_ref, dense, rows,
):
    spread_kernel(tiles, first, place, z_ref, y_ref, dense)
    total = acc_ref[...] + meet((a0, a1, a2, a3), tiles, first, rows, dense)
    encode(total[3 * BLK :], cross_ref)
    encode(total[2 * BLK : 3 * BLK], same_ref)
    keep_ref[...] = total[:BLK]
    upper_ref[...] = total[BLK : BLK + BLK // 2]
    lower_ref[...] = total[BLK + BLK // 2 : 2 * BLK]


def join_kernel(keep_ref, upper_ref, lower_ref, same_ref, cross_ref, out_ref):
    pair = lax.axis_index("pair")
    width = keep_ref.shape[1]
    across, groups, high = width // LANES, width // GROUP, same_ref.shape[1]
    for side, bases, coded in (
        (pair, (keep_ref,), same_ref),
        (1 - pair, (upper_ref, lower_ref), cross_ref),
    ):
        exps = coded[coded.shape[0] - 1].astype(jnp.int32).astype(jnp.float32)
        for i in range(BLK // high):
            base = bases[i * high // bases[0].shape[0]]
            at = i * high % bases[0].shape[0]
            for g in range(groups):
                n = i * groups + g
                scale = jnp.exp2(exps[:, n : n + 1] - 15.0)
                for k in range(GROUP // LANES):
                    s = g * (GROUP // LANES) + k
                    value = coded[i * across + s].astype(jnp.int32).astype(jnp.float32) * scale
                    where = pl.ds(pl.multiple_of(side * width + s * LANES, LANES), LANES)
                    out_ref[i * high : (i + 1) * high, where] = (
                        base[at : at + high, s * LANES : (s + 1) * LANES] + value
                    )


def call(kernel, out, operands, places, scratch=(), room=32):
    specs = {"s": SMEM, "v": VMEM, "a": pl.BlockSpec(memory_space=pltpu.HBM)}
    return pl.pallas_call(
        kernel,
        out_shape=out,
        in_specs=[specs[p] for p in places],
        out_specs=jax.tree.map(lambda _: VMEM, out),
        scratch_shapes=list(scratch),
        compiler_params=pltpu.CompilerParams(vmem_limit_bytes=room * MIB),
        cost_estimate=pl.CostEstimate(flops=1, bytes_accessed=1, transcendentals=0),
    )(*operands)


def swap_body(amplitudes, integrals, tile_list, slab_order, block_list):
    wide_count, pair_count = lax.axis_size("wide"), lax.axis_size("pair")
    depth, width = integrals.shape
    tiles, group = depth // BLK, width // BLK
    keep = block_list.shape[2]
    bf16, f32, i16, i32 = jnp.bfloat16, jnp.float32, jnp.int16, jnp.int32
    sds = jax.ShapeDtypeStruct
    bind = functools.partial

    def move(x, flip_wide, flip_pair=0):
        if flip_wide and flip_pair:
            n = wide_count * pair_count
            flip = flip_wide * pair_count + flip_pair
            return lax.ppermute(x, ("wide", "pair"), [(i, i ^ flip) for i in range(n)])
        if flip_wide:
            return lax.ppermute(x, "wide", [(i, i ^ flip_wide) for i in range(wide_count)])
        return lax.ppermute(x, "pair", [(i, i ^ flip_pair) for i in range(pair_count)])

    lists = block_list.transpose(2, 1, 0)

    head = SPLIT
    tail = tiles - head
    first, second = call(
        pack_kernel,
        tuple(sds((count * BLK, keep * BLK), bf16) for count in (head, tail)),
        (lists, integrals),
        "aa",
        [
            pltpu.SMEM(lists.shape, i32),
            pltpu.VMEM(integrals.shape, bf16),
            pltpu.SemaphoreType.DMA((tiles + 1,)),
        ],
        ROOM,
    )
    own, far = call(
        mask_kernel,
        (sds((BLK, amplitudes.shape[1] // 2), bf16),) * 2,
        (tile_list, slab_order, amplitudes),
        "aaa",
        [
            pltpu.SMEM(tile_list.shape, i32),
            pltpu.SMEM(slab_order.shape, i32),
            pltpu.VMEM(amplitudes.shape, bf16),
            pltpu.SMEM((amplitudes.shape[1] // BLK,), i32),
            pltpu.SemaphoreType.DMA((3,)),
        ],
        ROOM,
    )
    z_first = move(first, 2)
    z_second = move(second, 2)
    far_same = move(far, 4)
    near = move(integrals, 1)
    own_cross = move(own, 0, 1)
    far_cross = move(far_same, 0, 1)

    my_lists = lax.dynamic_index_in_dim(block_list, lax.axis_index("pair"), 1, keepdims=False)
    hit = my_lists[:, :, None] == jnp.arange(group, dtype=i32)[None, None, :]
    order = jnp.arange(1, keep + 1, dtype=i32)[None, :, None]
    place = (jnp.sum(jnp.where(hit, order, 0), axis=1) - 1).reshape(-1)

    raw = call(raw_kernel, sds((2 * depth, width), bf16), (place, integrals, near), "svv")
    y_first = move(z_first, 1)
    amps = (own, own_cross, far_same, far_cross)
    rows = len(amps) * BLK
    raw_rows = pltpu.VMEM((rows, 2 * depth), bf16)

    def scratch(count):
        return pltpu.VMEM((rows, 2 * count * BLK), bf16)

    dense_first = call(
        bind(spread_kernel, tiles, 0),
        sds((2 * head * BLK, width), bf16),
        (place, z_first, y_first),
        "svv",
    )
    acc = call(
        bind(early_kernel, tiles),
        sds((rows, width), f32),
        (raw, dense_first, *amps),
        "v" * 6,
        [raw_rows, scratch(head)],
    )
    z_second, acc = lax.optimization_barrier((z_second, acc))
    y_second = move(z_second, 1)
    coded = sds((BLK * width // (16 * LANES) + 1, 16, LANES), i16)
    part = sds((BLK // 2, width), f32)
    keep_rows, upper, lower, same, cross = call(
        bind(last_kernel, tiles, head),
        (sds((BLK, width), f32), part, part, coded, coded),
        (place, z_second, y_second, *amps, acc),
        "s" + "v" * 7,
        [pltpu.VMEM((2 * tail * BLK, width), bf16), scratch(tail)],
    )
    got_cross = move(cross, 4, 1)
    got_same = move(same, 4)
    return call(
        join_kernel,
        sds((BLK, pair_count * width), f32),
        (keep_rows, move(upper, 0, 1), move(lower, 0, 1), got_same, got_cross),
        "v" * 5,
    )


def solution(mesh):
    placed = (
        P(("grp", "wide", "pair"), None),
        P(("grp", "wide"), "pair"),
        P("grp", None),
        P("grp"),
        P("grp", None, None),
    )
    swapped = mesh.shape["wide"] == 8 and mesh.shape["pair"] == 2
    return jax.shard_map(
        swap_body if swapped else gather_body,
        mesh=mesh,
        in_specs=placed,
        out_specs=P(("grp", "wide", "pair"), None),
        check_vma=False,
    )
```

```python
import functools

import jax
import jax.numpy as jnp
from jax import lax
from jax.experimental import pallas as pl
from jax.experimental.pallas import tpu as pltpu
from jax.sharding import PartitionSpec as P

BLK = 64
LANES = 128
GROUP = 256
LOW_EXP = -100.0
ROOM = 60
PIECE = 192
SPLIT = 3
VMEM = pl.BlockSpec(memory_space=pltpu.VMEM)
SMEM = pl.BlockSpec(memory_space=pltpu.SMEM)
MIB = 1024 * 1024


def gather_body(amplitudes, integrals, tile_list, slab_order, block_list):
    rows_dev, virt_cols = amplitudes.shape
    virt_tiles = virt_cols // BLK
    own_count = rows_dev // BLK
    pair_count = lax.axis_size("pair")
    group_count = own_count * pair_count
    wide_index = lax.axis_index("wide")
    pair_index = lax.axis_index("pair")
    slab_ids = lax.dynamic_slice_in_dim(slab_order, wide_index * group_count, group_count)
    own_ids = lax.dynamic_slice_in_dim(slab_ids, pair_index * own_count, own_count)
    own_lists = jnp.take(tile_list, own_ids, axis=0)
    tiles_four = amplitudes.reshape(own_count, BLK, virt_tiles, BLK)
    tile_ids = jnp.arange(virt_tiles, dtype=jnp.int32)
    present = jnp.any(own_lists[:, :, None] == tile_ids[None, None, :], axis=1).astype(
        amplitudes.dtype
    )
    masked = (tiles_four * present[:, None, :, None]).reshape(rows_dev, virt_cols)
    slab_rows = lax.all_gather(masked, "pair", axis=0, tiled=True)
    group_tiles = integrals.shape[1] // BLK
    my_lists = lax.dynamic_index_in_dim(block_list, pair_index, 1, keepdims=False)
    group_ids = jnp.arange(group_tiles, dtype=jnp.int32)
    live = jnp.any(my_lists[:, :, None] == group_ids[None, None, :], axis=1).astype(integrals.dtype)
    shard_block = lax.all_gather(integrals, "wide", axis=0, tiled=True)
    qtiles = shard_block.shape[0] // BLK
    masked_block = shard_block.reshape(qtiles, BLK, group_tiles, BLK) * live[:, None, :, None]
    masked_block = masked_block.reshape(shard_block.shape)
    ladder_slab = jnp.dot(slab_rows, masked_block, preferred_element_type=jnp.float32)
    return lax.all_to_all(ladder_slab, "pair", split_axis=0, concat_axis=1, tiled=True)


def low_lanes(rows):
    return lax.broadcasted_iota(jnp.int32, (rows, LANES), 1) < BLK


def half(index):
    return pl.ds(pl.multiple_of((index // 2) * LANES, LANES), LANES)


def fetch(pairs, sems):
    copies = [pltpu.make_async_copy(s, d, sems.at[n]) for n, (s, d) in enumerate(pairs)]
    for copy in copies:
        copy.start()
    return copies


def pack_kernel(lists_ref, block_ref, first_ref, second_ref, lists, block, sems):
    wide, pair = lax.axis_index("wide"), lax.axis_index("pair")
    tiles = block_ref.shape[0] // BLK
    keep = first_ref.shape[1] // BLK
    split = first_ref.shape[0] // BLK
    rows = [pl.ds(i * BLK, BLK) for i in range(tiles)]
    copies = fetch([(lists_ref, lists)] + [(block_ref.at[r], block.at[r]) for r in rows], sems)
    copies[0].wait()
    low = low_lanes(BLK)
    for i in range(tiles):
        copies[1 + i].wait()
        out, row = (first_ref, i) if i < split else (second_ref, i - split)
        u = wide * tiles + i
        for j in range(keep // 2):
            even, odd = lists[2 * j, pair, u], lists[2 * j + 1, pair, u]
            left = pltpu.roll(block[rows[i], half(even)], (even % 2) * BLK, 1)
            right = pltpu.roll(block[rows[i], half(odd)], BLK - (odd % 2) * BLK, 1)
            out[row * BLK : (row + 1) * BLK, j * LANES : (j + 1) * LANES] = jnp.where(
                low, left, right
            )


def raw_kernel(place, own_ref, near_ref, dense):
    wide = lax.axis_index("wide")
    depth, width = own_ref.shape
    tiles, group = depth // BLK, width // BLK
    low = low_lanes(BLK)
    for block, source in ((own_ref, wide), (near_ref, wide ^ 1)):
        for i in range(tiles):
            base = (source * tiles + i) * group
            here = pl.ds(pl.multiple_of((source % 2) * depth + i * BLK, BLK), BLK)
            for s in range(group // 2):
                cols = slice(s * LANES, (s + 1) * LANES)
                flag = jnp.where(low, place[base + 2 * s], place[base + 2 * s + 1])
                dense[here, cols] = jnp.where(flag >= 0, block[i * BLK : (i + 1) * BLK, cols], 0)


def spread(place, packed, dense, source_row):
    tiles = packed.shape[0] // BLK
    group = dense.shape[1] // BLK
    low = low_lanes(BLK)
    for i in range(tiles):
        here = slice(i * BLK, (i + 1) * BLK)
        base = (source_row + i) * group
        for s in range(group // 2):
            even, odd = place[base + 2 * s], place[base + 2 * s + 1]
            left_at, right_at = jnp.maximum(even, 0), jnp.maximum(odd, 0)
            left = pltpu.roll(packed[here, half(left_at)], (left_at % 2) * BLK, 1)
            right = pltpu.roll(packed[here, half(right_at)], BLK - (right_at % 2) * BLK, 1)
            flag = jnp.where(low, even, odd)
            dense[here, s * LANES : (s + 1) * LANES] = jnp.where(
                flag >= 0, jnp.where(low, left, right), 0
            )


def mask_kernel(
    tiles, head, tile_ref, slab_ref, amp_ref, own, far, tile_list, slab, amp, present, sems
):
    wide, pair = lax.axis_index("wide"), lax.axis_index("pair")
    copies = fetch([(tile_ref, tile_list), (slab_ref, slab), (amp_ref, amp)], sems)
    count = amp_ref.shape[1] // BLK
    for t in range(count):
        present[t] = 0
    copies[0].wait()
    copies[1].wait()
    tile = slab[wide * 2 + pair]
    for k in range(tile_list.shape[1]):
        present[tile_list[tile, k]] = 1
    chip = ((wide // 2) % 2) * 2 * tiles
    order = [chip + t for t in range(2 * tiles)]
    for first, last in ((0, head), (head, tiles)):
        for source in (wide ^ 2, wide ^ 3):
            order += [(source % 4) * tiles + t for t in range(first, last)]
    low = low_lanes(BLK)
    copies[2].wait()
    for side, out in ((1 - wide // 4, far), (wide // 4, own)):
        base = side * (count // 2)
        for b in range(count // 4):
            even, odd = base + order[2 * b], base + order[2 * b + 1]
            left = pltpu.roll(amp[:, half(even)], (even % 2) * BLK, 1)
            right = pltpu.roll(amp[:, half(odd)], BLK - (odd % 2) * BLK, 1)
            flag = jnp.where(low, present[even], present[odd])
            out[:, b * LANES : (b + 1) * LANES] = jnp.where(
                flag > 0, jnp.where(low, left, right), 0
            )


def dot(a, b):
    return jnp.dot(a, b, preferred_element_type=jnp.float32)


def first_kernel(tiles, place, z_ref, *rest):
    wide = lax.axis_index("wide")
    y_refs, dense = rest[:-1], rest[-1]
    row = 0
    for blocks, source in (((z_ref,), wide ^ 2), (y_refs, wide ^ 3)):
        tile = source * tiles
        for block in blocks:
            size = block.shape[0]
            spread(place, block, dense.at[row : row + size], tile)
            row, tile = row + size, tile + size // BLK


def second_kernel(tiles, first, place, z_ref, dense):
    spread(place, z_ref, dense, (lax.axis_index("wide") ^ 2) * tiles + first)


def early_kernel(raw, dense, rows, acc_ref):
    depth = raw.shape[0]
    acc_ref[...] = dot(rows[:, :depth], raw[...]) + dot(
        rows[:, depth : depth + dense.shape[0]], dense[...]
    )


def encode(values, out):
    width = values.shape[1]
    across = width // LANES
    high = out.shape[1]
    groups = width // GROUP
    lane = lax.broadcasted_iota(jnp.int32, (high, LANES), 1)
    exps = jnp.zeros((high, LANES), jnp.int32)
    for i in range(BLK // high):
        for g in range(groups):
            part = values[i * high : (i + 1) * high, g * GROUP : (g + 1) * GROUP]
            top = jnp.max(jnp.abs(part), axis=1, keepdims=True)
            exp = jnp.maximum(jnp.ceil(jnp.log2(jnp.maximum(top, 2.0**LOW_EXP))), LOW_EXP)
            scaled = jnp.clip(jnp.round(part * jnp.exp2(15.0 - exp)), -32767.0, 32767.0)
            coded = scaled.astype(jnp.int32).astype(jnp.int16)
            for k in range(GROUP // LANES):
                at = i * across + g * (GROUP // LANES) + k
                out[at] = coded[:, k * LANES : (k + 1) * LANES]
            exps = jnp.where(lane == i * groups + g, exp.astype(jnp.int32), exps)
    out[out.shape[0] - 1] = exps.astype(jnp.int16)


def last_kernel(
    tiles, first, place, y_ref, z_dense, rows, far_cross, acc, cross_acc, keep_ref, upper_ref,
    lower_ref, same_ref, cross_ref, dense,
):
    depth = z_dense.shape[0]
    dense[:depth] = z_dense[...]
    source = lax.axis_index("wide") ^ 3
    spread(place, y_ref, dense.at[depth : 2 * depth], source * tiles + first)
    at = rows.shape[1] - 2 * depth
    encode(cross_acc[...] + dot(far_cross[:, at:], dense[...]), cross_ref)
    total = acc[...] + dot(rows[:, at:], dense[...])
    encode(total[2 * BLK :], same_ref)
    keep_ref[...] = total[:BLK]
    upper_ref[...] = total[BLK : BLK + BLK // 2]
    lower_ref[...] = total[BLK + BLK // 2 : 2 * BLK]


def join_kernel(keep_ref, upper_ref, lower_ref, same_ref, cross_ref, out_ref):
    pair = lax.axis_index("pair")
    width = keep_ref.shape[1]
    across, groups, high = width // LANES, width // GROUP, same_ref.shape[1]
    for side, bases, coded in (
        (pair, (keep_ref,), same_ref),
        (1 - pair, (upper_ref, lower_ref), cross_ref),
    ):
        exps = coded[coded.shape[0] - 1].astype(jnp.int32).astype(jnp.float32)
        for i in range(BLK // high):
            base = bases[i * high // bases[0].shape[0]]
            at = i * high % bases[0].shape[0]
            for g in range(groups):
                n = i * groups + g
                scale = jnp.exp2(exps[:, n : n + 1] - 15.0)
                for k in range(GROUP // LANES):
                    s = g * (GROUP // LANES) + k
                    value = coded[i * across + s].astype(jnp.int32).astype(jnp.float32) * scale
                    where = pl.ds(pl.multiple_of(side * width + s * LANES, LANES), LANES)
                    out_ref[i * high : (i + 1) * high, where] = (
                        base[at : at + high, s * LANES : (s + 1) * LANES] + value
                    )


def call(kernel, out, operands, places, scratch=(), room=32):
    specs = {"s": SMEM, "v": VMEM, "a": pl.BlockSpec(memory_space=pltpu.HBM)}
    return pl.pallas_call(
        kernel,
        out_shape=out,
        in_specs=[specs[p] for p in places],
        out_specs=jax.tree.map(lambda _: VMEM, out),
        scratch_shapes=list(scratch),
        compiler_params=pltpu.CompilerParams(vmem_limit_bytes=room * MIB),
        cost_estimate=pl.CostEstimate(flops=1, bytes_accessed=1, transcendentals=0),
    )(*operands)


def swap_body(amplitudes, integrals, tile_list, slab_order, block_list):
    wide_count, pair_count = lax.axis_size("wide"), lax.axis_size("pair")
    depth, width = integrals.shape
    tiles, group = depth // BLK, width // BLK
    keep = block_list.shape[2]
    bf16, f32, i16, i32 = jnp.bfloat16, jnp.float32, jnp.int16, jnp.int32
    sds = jax.ShapeDtypeStruct
    bind = functools.partial

    def move(x, flip_wide, flip_pair=0):
        if flip_wide and flip_pair:
            n = wide_count * pair_count
            flip = flip_wide * pair_count + flip_pair
            return lax.ppermute(x, ("wide", "pair"), [(i, i ^ flip) for i in range(n)])
        if flip_wide:
            return lax.ppermute(x, "wide", [(i, i ^ flip_wide) for i in range(wide_count)])
        return lax.ppermute(x, "pair", [(i, i ^ flip_pair) for i in range(pair_count)])

    lists = block_list.transpose(2, 1, 0)

    head = SPLIT
    tail = tiles - head

    first, second = call(
        pack_kernel,
        tuple(sds((count * BLK, keep * BLK), bf16) for count in (head, tail)),
        (lists, integrals),
        "aa",
        [
            pltpu.SMEM(lists.shape, i32),
            pltpu.VMEM(integrals.shape, bf16),
            pltpu.SemaphoreType.DMA((tiles + 1,)),
        ],
        ROOM,
    )
    cols = amplitudes.shape[1] // 2
    own, far = call(
        bind(mask_kernel, tiles, head),
        (sds((BLK, cols), bf16),) * 2,
        (tile_list, slab_order, amplitudes),
        "aaa",
        [
            pltpu.SMEM(tile_list.shape, i32),
            pltpu.SMEM(slab_order.shape, i32),
            pltpu.VMEM(amplitudes.shape, bf16),
            pltpu.SMEM((2 * cols // BLK,), i32),
            pltpu.SemaphoreType.DMA((3,)),
        ],
        ROOM,
    )
    z_first = move(first, 2)
    z_second = move(second, 2)
    far_same = move(far, 4)
    near = move(integrals, 1)
    own_cross = move(own, 0, 1)
    far_cross = move(far_same, 0, 1)

    my_lists = lax.dynamic_index_in_dim(block_list, lax.axis_index("pair"), 1, keepdims=False)
    hit = my_lists[:, :, None] == jnp.arange(group, dtype=i32)[None, None, :]
    order = jnp.arange(1, keep + 1, dtype=i32)[None, :, None]
    place = (jnp.sum(jnp.where(hit, order, 0), axis=1) - 1).reshape(-1)

    raw = call(raw_kernel, sds((2 * depth, width), bf16), (place, integrals, near), "svv")
    y_first = [move(z_first[a : a + PIECE], 1) for a in range(0, head * BLK, PIECE)]
    y_first[0], own_cross = lax.optimization_barrier((y_first[0], own_cross))
    dense_first = call(
        bind(first_kernel, tiles),
        sds((2 * head * BLK, width), bf16),
        (place, z_first, *y_first),
        "sv" + "v" * len(y_first),
    )

    def begin(rows):
        return call(early_kernel, sds((rows.shape[0], width), f32), (raw, dense_first, rows), "vvv")

    rows = jnp.concatenate((own, own_cross, far_same), axis=0)
    acc = begin(rows)
    far_cross, acc = lax.optimization_barrier((far_cross, acc))
    cross_acc = begin(far_cross)
    z_second, cross_acc = lax.optimization_barrier((z_second, cross_acc))
    y_second = move(z_second, 1)
    z_dense = call(
        bind(second_kernel, tiles, head),
        sds((tail * BLK, width), bf16),
        (place, z_second),
        "sv",
    )
    coded = sds((BLK * width // (16 * LANES) + 1, 16, LANES), i16)
    part = sds((BLK // 2, width), f32)
    keep_rows, upper, lower, same, cross = call(
        bind(last_kernel, tiles, head),
        (sds((BLK, width), f32), part, part, coded, coded),
        (place, y_second, z_dense, rows, far_cross, acc, cross_acc),
        "svvvvvv",
        [pltpu.VMEM((2 * tail * BLK, width), bf16)],
    )
    got_cross = move(cross, 4, 1)
    got_same = move(same, 4)
    return call(
        join_kernel,
        sds((BLK, pair_count * width), f32),
        (keep_rows, move(upper, 0, 1), move(lower, 0, 1), got_same, got_cross),
        "v" * 5,
    )


def solution(mesh):
    placed = (
        P(("grp", "wide", "pair"), None),
        P(("grp", "wide"), "pair"),
        P("grp", None),
        P("grp"),
        P("grp", None, None),
    )
    swapped = mesh.shape["wide"] == 8 and mesh.shape["pair"] == 2
    return jax.shard_map(
        swap_body if swapped else gather_body,
        mesh=mesh,
        in_specs=placed,
        out_specs=P(("grp", "wide", "pair"), None),
        check_vma=False,
    )
```

```python
import functools

import jax
import jax.numpy as jnp
from jax import lax
from jax.experimental import pallas as pl
from jax.experimental.pallas import tpu as pltpu
from jax.sharding import PartitionSpec as P

BLK = 64
LANES = 128
GROUP = 256
LOW_EXP = -100.0
ROOM = 60
PIECE = 192
SPLIT = 3
VMEM = pl.BlockSpec(memory_space=pltpu.VMEM)
SMEM = pl.BlockSpec(memory_space=pltpu.SMEM)
MIB = 1024 * 1024


def gather_body(amplitudes, integrals, tile_list, slab_order, block_list):
    rows_dev, virt_cols = amplitudes.shape
    virt_tiles = virt_cols // BLK
    own_count = rows_dev // BLK
    pair_count = lax.axis_size("pair")
    group_count = own_count * pair_count
    wide_index = lax.axis_index("wide")
    pair_index = lax.axis_index("pair")
    slab_ids = lax.dynamic_slice_in_dim(slab_order, wide_index * group_count, group_count)
    own_ids = lax.dynamic_slice_in_dim(slab_ids, pair_index * own_count, own_count)
    own_lists = jnp.take(tile_list, own_ids, axis=0)
    tiles_four = amplitudes.reshape(own_count, BLK, virt_tiles, BLK)
    tile_ids = jnp.arange(virt_tiles, dtype=jnp.int32)
    present = jnp.any(own_lists[:, :, None] == tile_ids[None, None, :], axis=1).astype(
        amplitudes.dtype
    )
    masked = (tiles_four * present[:, None, :, None]).reshape(rows_dev, virt_cols)
    slab_rows = lax.all_gather(masked, "pair", axis=0, tiled=True)
    group_tiles = integrals.shape[1] // BLK
    my_lists = lax.dynamic_index_in_dim(block_list, pair_index, 1, keepdims=False)
    group_ids = jnp.arange(group_tiles, dtype=jnp.int32)
    live = jnp.any(my_lists[:, :, None] == group_ids[None, None, :], axis=1).astype(integrals.dtype)
    shard_block = lax.all_gather(integrals, "wide", axis=0, tiled=True)
    qtiles = shard_block.shape[0] // BLK
    masked_block = shard_block.reshape(qtiles, BLK, group_tiles, BLK) * live[:, None, :, None]
    masked_block = masked_block.reshape(shard_block.shape)
    ladder_slab = jnp.dot(slab_rows, masked_block, preferred_element_type=jnp.float32)
    return lax.all_to_all(ladder_slab, "pair", split_axis=0, concat_axis=1, tiled=True)


def low_lanes(rows):
    return lax.broadcasted_iota(jnp.int32, (rows, LANES), 1) < BLK


def half(index):
    return pl.ds(pl.multiple_of((index // 2) * LANES, LANES), LANES)


def fetch(pairs, sems):
    copies = [pltpu.make_async_copy(s, d, sems.at[n]) for n, (s, d) in enumerate(pairs)]
    for copy in copies:
        copy.start()
    return copies


def pack_kernel(start, lists_ref, block_ref, out, lists, block, sems):
    wide, pair = lax.axis_index("wide"), lax.axis_index("pair")
    tiles = block_ref.shape[0] // BLK
    keep = out.shape[1] // BLK
    count = out.shape[0] // BLK
    rows = [pl.ds(i * BLK, BLK) for i in range(count)]
    sources = [block_ref.at[pl.ds((start + i) * BLK, BLK)] for i in range(count)]
    copies = fetch(
        [(lists_ref, lists)] + [(s, block.at[r]) for s, r in zip(sources, rows)], sems
    )
    copies[0].wait()
    low = low_lanes(BLK)
    for i in range(count):
        copies[1 + i].wait()
        u = wide * tiles + start + i
        for j in range(keep // 2):
            even, odd = lists[2 * j, pair, u], lists[2 * j + 1, pair, u]
            left = pltpu.roll(block[rows[i], half(even)], (even % 2) * BLK, 1)
            right = pltpu.roll(block[rows[i], half(odd)], BLK - (odd % 2) * BLK, 1)
            out[rows[i], j * LANES : (j + 1) * LANES] = jnp.where(low, left, right)


def raw_kernel(place, own_ref, near_ref, dense):
    wide = lax.axis_index("wide")
    depth, width = own_ref.shape
    tiles, group = depth // BLK, width // BLK
    low = low_lanes(BLK)
    for block, source in ((own_ref, wide), (near_ref, wide ^ 1)):
        for i in range(tiles):
            base = (source * tiles + i) * group
            here = pl.ds(pl.multiple_of((source % 2) * depth + i * BLK, BLK), BLK)
            for s in range(group // 2):
                cols = slice(s * LANES, (s + 1) * LANES)
                flag = jnp.where(low, place[base + 2 * s], place[base + 2 * s + 1])
                dense[here, cols] = jnp.where(flag >= 0, block[i * BLK : (i + 1) * BLK, cols], 0)


def spread(place, packed, dense, source_row):
    tiles = packed.shape[0] // BLK
    group = dense.shape[1] // BLK
    low = low_lanes(BLK)
    for i in range(tiles):
        here = slice(i * BLK, (i + 1) * BLK)
        base = (source_row + i) * group
        for s in range(group // 2):
            even, odd = place[base + 2 * s], place[base + 2 * s + 1]
            left_at, right_at = jnp.maximum(even, 0), jnp.maximum(odd, 0)
            left = pltpu.roll(packed[here, half(left_at)], (left_at % 2) * BLK, 1)
            right = pltpu.roll(packed[here, half(right_at)], BLK - (right_at % 2) * BLK, 1)
            flag = jnp.where(low, even, odd)
            dense[here, s * LANES : (s + 1) * LANES] = jnp.where(
                flag >= 0, jnp.where(low, left, right), 0
            )


def mask_kernel(
    tiles, head, tile_ref, slab_ref, amp_ref, own, far, tile_list, slab, amp, present, sems
):
    wide, pair = lax.axis_index("wide"), lax.axis_index("pair")
    copies = fetch([(tile_ref, tile_list), (slab_ref, slab), (amp_ref, amp)], sems)
    count = amp_ref.shape[1] // BLK
    for t in range(count):
        present[t] = 0
    copies[0].wait()
    copies[1].wait()
    tile = slab[wide * 2 + pair]
    for k in range(tile_list.shape[1]):
        present[tile_list[tile, k]] = 1
    chip = ((wide // 2) % 2) * 2 * tiles
    order = [chip + t for t in range(2 * tiles)]
    for first, last in ((0, head), (head, tiles)):
        for source in (wide ^ 2, wide ^ 3):
            order += [(source % 4) * tiles + t for t in range(first, last)]
    low = low_lanes(BLK)
    copies[2].wait()
    for side, out in ((1 - wide // 4, far), (wide // 4, own)):
        base = side * (count // 2)
        for b in range(count // 4):
            even, odd = base + order[2 * b], base + order[2 * b + 1]
            left = pltpu.roll(amp[:, half(even)], (even % 2) * BLK, 1)
            right = pltpu.roll(amp[:, half(odd)], BLK - (odd % 2) * BLK, 1)
            flag = jnp.where(low, present[even], present[odd])
            out[:, b * LANES : (b + 1) * LANES] = jnp.where(
                flag > 0, jnp.where(low, left, right), 0
            )


def dot(a, b):
    return jnp.dot(a, b, preferred_element_type=jnp.float32)


def first_kernel(tiles, place, z_ref, *rest):
    wide = lax.axis_index("wide")
    y_refs, dense = rest[:-1], rest[-1]
    row = 0
    for blocks, source in (((z_ref,), wide ^ 2), (y_refs, wide ^ 3)):
        tile = source * tiles
        for block in blocks:
            size = block.shape[0]
            spread(place, block, dense.at[row : row + size], tile)
            row, tile = row + size, tile + size // BLK


def second_kernel(tiles, first, place, z_ref, dense):
    spread(place, z_ref, dense, (lax.axis_index("wide") ^ 2) * tiles + first)


def early_kernel(raw, dense, rows, acc_ref):
    depth = raw.shape[0]
    acc_ref[...] = dot(rows[:, :depth], raw[...]) + dot(
        rows[:, depth : depth + dense.shape[0]], dense[...]
    )


def encode(values, out):
    width = values.shape[1]
    across = width // LANES
    high = out.shape[1]
    groups = width // GROUP
    lane = lax.broadcasted_iota(jnp.int32, (high, LANES), 1)
    exps = jnp.zeros((high, LANES), jnp.int32)
    for i in range(BLK // high):
        for g in range(groups):
            part = values[i * high : (i + 1) * high, g * GROUP : (g + 1) * GROUP]
            top = jnp.max(jnp.abs(part), axis=1, keepdims=True)
            exp = jnp.maximum(jnp.ceil(jnp.log2(jnp.maximum(top, 2.0**LOW_EXP))), LOW_EXP)
            scaled = jnp.clip(jnp.round(part * jnp.exp2(15.0 - exp)), -32767.0, 32767.0)
            coded = scaled.astype(jnp.int32).astype(jnp.int16)
            for k in range(GROUP // LANES):
                at = i * across + g * (GROUP // LANES) + k
                out[at] = coded[:, k * LANES : (k + 1) * LANES]
            exps = jnp.where(lane == i * groups + g, exp.astype(jnp.int32), exps)
    for n in range(BLK // high * across, out.shape[0]):
        out[n] = exps.astype(jnp.int16)


def cross_kernel(tiles, first, place, y_ref, z_dense, rows, acc, coded, y_dense):
    spread(place, y_ref, y_dense, (lax.axis_index("wide") ^ 3) * tiles + first)
    encode(acc[...] + finish(rows[...], z_dense, y_dense), coded)


def finish(rows, z_dense, y_dense):
    depth = z_dense.shape[0]
    at = rows.shape[1] - 2 * depth
    return dot(rows[:, at : at + depth], z_dense[...]) + dot(rows[:, at + depth :], y_dense[...])


def same_kernel(z_dense, y_dense, rows, acc, coded):
    here = slice(2 * BLK, 3 * BLK)
    encode(acc[here] + finish(rows[here], z_dense, y_dense), coded)


def own_kernel(z_dense, y_dense, rows, acc, _, keep_ref, upper_ref, lower_ref):
    here = slice(0, 2 * BLK)
    total = acc[here] + finish(rows[here], z_dense, y_dense)
    keep_ref[...] = total[:BLK]
    upper_ref[...] = total[BLK : BLK + BLK // 2]
    lower_ref[...] = total[BLK + BLK // 2 :]


def join_kernel(flip, coded, *rest):
    bases, (out_ref, whole, sems) = rest[:-3], rest[-3:]
    bases = bases[-2:] if flip else bases[-1:]
    pair = lax.axis_index("pair") ^ flip
    width = whole.shape[1]
    across, groups, high = width // LANES, width // GROUP, coded.shape[1]
    cols = pl.ds(pl.multiple_of(pair * width, LANES), width)
    exps = coded[BLK // high * across].astype(jnp.int32).astype(jnp.float32)
    copies = []
    for i in range(BLK // high):
        base = bases[i * high // bases[0].shape[0]]
        at = i * high % bases[0].shape[0]
        for g in range(groups):
            n = i * groups + g
            scale = jnp.exp2(exps[:, n : n + 1] - 15.0)
            for k in range(GROUP // LANES):
                s = g * (GROUP // LANES) + k
                here = slice(s * LANES, (s + 1) * LANES)
                value = coded[i * across + s].astype(jnp.int32).astype(jnp.float32) * scale
                whole[i * high : (i + 1) * high, here] = base[at : at + high, here] + value
        here = pl.ds(i * high, high)
        copies.append(pltpu.make_async_copy(whole.at[here], out_ref.at[here, cols], sems.at[i]))
        copies[-1].start()
    for copy in copies:
        copy.wait()


def call(kernel, out, operands, places, scratch=(), room=32, **options):
    specs = {"s": SMEM, "v": VMEM, "a": pl.BlockSpec(memory_space=pltpu.HBM)}
    return pl.pallas_call(
        kernel,
        out_shape=out,
        in_specs=[specs[p] for p in places],
        scratch_shapes=list(scratch),
        compiler_params=pltpu.CompilerParams(vmem_limit_bytes=room * MIB),
        cost_estimate=pl.CostEstimate(flops=1, bytes_accessed=1, transcendentals=0),
        **{"out_specs": jax.tree.map(lambda _: VMEM, out), **options},
    )(*operands)


def swap_body(amplitudes, integrals, tile_list, slab_order, block_list):
    wide_count, pair_count = lax.axis_size("wide"), lax.axis_size("pair")
    depth, width = integrals.shape
    tiles, group = depth // BLK, width // BLK
    keep = block_list.shape[2]
    bf16, f32, i16, i32 = jnp.bfloat16, jnp.float32, jnp.int16, jnp.int32
    sds = jax.ShapeDtypeStruct
    bind = functools.partial

    def move(x, flip_wide, flip_pair=0):
        if flip_wide and flip_pair:
            n = wide_count * pair_count
            flip = flip_wide * pair_count + flip_pair
            return lax.ppermute(x, ("wide", "pair"), [(i, i ^ flip) for i in range(n)])
        if flip_wide:
            return lax.ppermute(x, "wide", [(i, i ^ flip_wide) for i in range(wide_count)])
        return lax.ppermute(x, "pair", [(i, i ^ flip_pair) for i in range(pair_count)])

    lists = block_list.transpose(2, 1, 0)

    head = SPLIT
    tail = tiles - head

    def pack(start, count):
        return call(
            bind(pack_kernel, start),
            sds((count * BLK, keep * BLK), bf16),
            (lists, integrals),
            "aa",
            [
                pltpu.SMEM(lists.shape, i32),
                pltpu.VMEM((count * BLK, width), bf16),
                pltpu.SemaphoreType.DMA((count + 1,)),
            ],
            ROOM,
        )

    cols = amplitudes.shape[1] // 2
    own, far = call(
        bind(mask_kernel, tiles, head),
        (sds((BLK, cols), bf16),) * 2,
        (tile_list, slab_order, amplitudes),
        "aaa",
        [
            pltpu.SMEM(tile_list.shape, i32),
            pltpu.SMEM(slab_order.shape, i32),
            pltpu.VMEM(amplitudes.shape, bf16),
            pltpu.SMEM((2 * cols // BLK,), i32),
            pltpu.SemaphoreType.DMA((3,)),
        ],
        ROOM,
    )
    z_first = move(pack(0, head), 2)
    z_second = move(pack(head, tail), 2)
    far_same = move(far, 4)
    near = move(integrals, 1)
    own_cross = move(own, 0, 1)
    far_cross = move(far_same, 0, 1)

    my_lists = lax.dynamic_index_in_dim(block_list, lax.axis_index("pair"), 1, keepdims=False)
    hit = my_lists[:, :, None] == jnp.arange(group, dtype=i32)[None, None, :]
    order = jnp.arange(1, keep + 1, dtype=i32)[None, :, None]
    place = (jnp.sum(jnp.where(hit, order, 0), axis=1) - 1).reshape(-1)

    raw = call(raw_kernel, sds((2 * depth, width), bf16), (place, integrals, near), "svv")
    y_first = [move(z_first[a : a + PIECE], 1) for a in range(0, head * BLK, PIECE)]
    y_first[0], own_cross = lax.optimization_barrier((y_first[0], own_cross))
    dense_first = call(
        bind(first_kernel, tiles),
        sds((2 * head * BLK, width), bf16),
        (place, z_first, *y_first),
        "sv" + "v" * len(y_first),
    )

    def begin(rows):
        return call(early_kernel, sds((rows.shape[0], width), f32), (raw, dense_first, rows), "vvv")

    rows = jnp.concatenate((own, own_cross, far_same), axis=0)
    acc = begin(rows)
    far_cross, acc = lax.optimization_barrier((far_cross, acc))
    cross_acc = begin(far_cross)
    z_second, cross_acc = lax.optimization_barrier((z_second, cross_acc))
    y_second = move(z_second, 1)
    z_dense = call(
        bind(second_kernel, tiles, head),
        sds((tail * BLK, width), bf16),
        (place, z_second),
        "sv",
    )
    coded = BLK * width // (16 * LANES) + 1
    part = sds((BLK // 2, width), f32)
    cross, y_dense = call(
        bind(cross_kernel, tiles, head),
        (sds((coded + 1, 16, LANES), i16), sds((tail * BLK, width), bf16)),
        (place, y_second, z_dense, far_cross, cross_acc),
        "svvvv",
    )
    got_cross = move(cross, 4, 1)
    same = call(
        same_kernel, sds((coded, 16, LANES), i16), (z_dense, y_dense, rows, acc), "vvvv"
    )
    got_same = move(same, 4)
    keep_rows, upper, lower = call(
        own_kernel,
        (sds((BLK, width), f32), part, part),
        (z_dense, y_dense, rows, acc, same),
        "vvvva",
    )

    def join(flip, coded, *bases):
        return call(
            bind(join_kernel, flip),
            sds((BLK, pair_count * width), f32),
            (coded, *bases),
            "v" + ("vv" if flip else "av"),
            [pltpu.VMEM((BLK, width), f32), pltpu.SemaphoreType.DMA((BLK // 16,))],
            out_specs=pl.BlockSpec(memory_space=pltpu.HBM),
            input_output_aliases={} if flip else {1: 0},
        )

    half_done = join(1, got_cross, move(upper, 0, 1), move(lower, 0, 1))
    return join(0, got_same, half_done, keep_rows)


def solution(mesh):
    placed = (
        P(("grp", "wide", "pair"), None),
        P(("grp", "wide"), "pair"),
        P("grp", None),
        P("grp"),
        P("grp", None, None),
    )
    swapped = mesh.shape["wide"] == 8 and mesh.shape["pair"] == 2
    return jax.shard_map(
        swap_body if swapped else gather_body,
        mesh=mesh,
        in_specs=placed,
        out_specs=P(("grp", "wide", "pair"), None),
        check_vma=False,
    )
```

```python
import functools

import jax
import jax.numpy as jnp
from jax import lax
from jax.experimental import pallas as pl
from jax.experimental.pallas import tpu as pltpu
from jax.sharding import PartitionSpec as P

BLK = 64
LANES = 128
GROUP = 256
LOW_EXP = -100.0
ROOM = 60
PIECE = 192
SPLIT = 3
VMEM = pl.BlockSpec(memory_space=pltpu.VMEM)
SMEM = pl.BlockSpec(memory_space=pltpu.SMEM)
MIB = 1024 * 1024


def gather_body(amplitudes, integrals, tile_list, slab_order, block_list):
    rows_dev, virt_cols = amplitudes.shape
    virt_tiles = virt_cols // BLK
    own_count = rows_dev // BLK
    pair_count = lax.axis_size("pair")
    group_count = own_count * pair_count
    wide_index = lax.axis_index("wide")
    pair_index = lax.axis_index("pair")
    slab_ids = lax.dynamic_slice_in_dim(slab_order, wide_index * group_count, group_count)
    own_ids = lax.dynamic_slice_in_dim(slab_ids, pair_index * own_count, own_count)
    own_lists = jnp.take(tile_list, own_ids, axis=0)
    tiles_four = amplitudes.reshape(own_count, BLK, virt_tiles, BLK)
    tile_ids = jnp.arange(virt_tiles, dtype=jnp.int32)
    present = jnp.any(own_lists[:, :, None] == tile_ids[None, None, :], axis=1).astype(
        amplitudes.dtype
    )
    masked = (tiles_four * present[:, None, :, None]).reshape(rows_dev, virt_cols)
    slab_rows = lax.all_gather(masked, "pair", axis=0, tiled=True)
    group_tiles = integrals.shape[1] // BLK
    my_lists = lax.dynamic_index_in_dim(block_list, pair_index, 1, keepdims=False)
    group_ids = jnp.arange(group_tiles, dtype=jnp.int32)
    live = jnp.any(my_lists[:, :, None] == group_ids[None, None, :], axis=1).astype(integrals.dtype)
    shard_block = lax.all_gather(integrals, "wide", axis=0, tiled=True)
    qtiles = shard_block.shape[0] // BLK
    masked_block = shard_block.reshape(qtiles, BLK, group_tiles, BLK) * live[:, None, :, None]
    masked_block = masked_block.reshape(shard_block.shape)
    ladder_slab = jnp.dot(slab_rows, masked_block, preferred_element_type=jnp.float32)
    return lax.all_to_all(ladder_slab, "pair", split_axis=0, concat_axis=1, tiled=True)


def low_lanes(rows):
    return lax.broadcasted_iota(jnp.int32, (rows, LANES), 1) < BLK


def half(index):
    return pl.ds(pl.multiple_of((index // 2) * LANES, LANES), LANES)


def fetch(pairs, sems):
    copies = [pltpu.make_async_copy(s, d, sems.at[n]) for n, (s, d) in enumerate(pairs)]
    for copy in copies:
        copy.start()
    return copies


def pack_kernel(start, lists_ref, block_ref, out, lists, block, sems):
    wide, pair = lax.axis_index("wide"), lax.axis_index("pair")
    tiles = block_ref.shape[0] // BLK
    keep = out.shape[1] // BLK
    count = out.shape[0] // BLK
    rows = [pl.ds(i * BLK, BLK) for i in range(count)]
    sources = [block_ref.at[pl.ds((start + i) * BLK, BLK)] for i in range(count)]
    copies = fetch(
        [(lists_ref, lists)] + [(s, block.at[r]) for s, r in zip(sources, rows)], sems
    )
    copies[0].wait()
    low = low_lanes(BLK)
    for i in range(count):
        copies[1 + i].wait()
        u = wide * tiles + start + i
        for j in range(keep // 2):
            even, odd = lists[2 * j, pair, u], lists[2 * j + 1, pair, u]
            left = pltpu.roll(block[rows[i], half(even)], (even % 2) * BLK, 1)
            right = pltpu.roll(block[rows[i], half(odd)], BLK - (odd % 2) * BLK, 1)
            out[rows[i], j * LANES : (j + 1) * LANES] = jnp.where(low, left, right)


def raw_kernel(place, own_ref, near_ref, dense):
    wide = lax.axis_index("wide")
    depth, width = own_ref.shape
    tiles, group = depth // BLK, width // BLK
    low = low_lanes(BLK)
    for block, source in ((own_ref, wide), (near_ref, wide ^ 1)):
        for i in range(tiles):
            base = (source * tiles + i) * group
            here = pl.ds(pl.multiple_of((source % 2) * depth + i * BLK, BLK), BLK)
            for s in range(group // 2):
                cols = slice(s * LANES, (s + 1) * LANES)
                flag = jnp.where(low, place[base + 2 * s], place[base + 2 * s + 1])
                dense[here, cols] = jnp.where(flag >= 0, block[i * BLK : (i + 1) * BLK, cols], 0)


def spread(place, packed, dense, source_row):
    tiles = packed.shape[0] // BLK
    group = dense.shape[1] // BLK
    low = low_lanes(BLK)
    for i in range(tiles):
        here = slice(i * BLK, (i + 1) * BLK)
        base = (source_row + i) * group
        for s in range(group // 2):
            even, odd = place[base + 2 * s], place[base + 2 * s + 1]
            left_at, right_at = jnp.maximum(even, 0), jnp.maximum(odd, 0)
            left = pltpu.roll(packed[here, half(left_at)], (left_at % 2) * BLK, 1)
            right = pltpu.roll(packed[here, half(right_at)], BLK - (right_at % 2) * BLK, 1)
            flag = jnp.where(low, even, odd)
            dense[here, s * LANES : (s + 1) * LANES] = jnp.where(
                flag >= 0, jnp.where(low, left, right), 0
            )


def mask_kernel(
    tiles, head, tile_ref, slab_ref, amp_ref, own, far, tile_list, slab, amp, present, sems
):
    wide, pair = lax.axis_index("wide"), lax.axis_index("pair")
    copies = fetch([(tile_ref, tile_list), (slab_ref, slab), (amp_ref, amp)], sems)
    count = amp_ref.shape[1] // BLK
    for t in range(count):
        present[t] = 0
    copies[0].wait()
    copies[1].wait()
    tile = slab[wide * 2 + pair]
    for k in range(tile_list.shape[1]):
        present[tile_list[tile, k]] = 1
    chip = ((wide // 2) % 2) * 2 * tiles
    order = [chip + t for t in range(2 * tiles)]
    for first, last in ((0, head), (head, tiles)):
        for source in (wide ^ 2, wide ^ 3):
            order += [(source % 4) * tiles + t for t in range(first, last)]
    low = low_lanes(BLK)
    copies[2].wait()
    for side, out in ((1 - wide // 4, far), (wide // 4, own)):
        base = side * (count // 2)
        for b in range(count // 4):
            even, odd = base + order[2 * b], base + order[2 * b + 1]
            left = pltpu.roll(amp[:, half(even)], (even % 2) * BLK, 1)
            right = pltpu.roll(amp[:, half(odd)], BLK - (odd % 2) * BLK, 1)
            flag = jnp.where(low, present[even], present[odd])
            out[:, b * LANES : (b + 1) * LANES] = jnp.where(
                flag > 0, jnp.where(low, left, right), 0
            )


def dot(a, b):
    return jnp.dot(a, b, preferred_element_type=jnp.float32)


def first_kernel(tiles, place, z_ref, *rest):
    wide = lax.axis_index("wide")
    y_refs, dense = rest[:-1], rest[-1]
    row = 0
    for blocks, source in (((z_ref,), wide ^ 2), (y_refs, wide ^ 3)):
        tile = source * tiles
        for block in blocks:
            size = block.shape[0]
            spread(place, block, dense.at[row : row + size], tile)
            row, tile = row + size, tile + size // BLK


def second_kernel(tiles, first, place, z_ref, dense):
    spread(place, z_ref, dense, (lax.axis_index("wide") ^ 2) * tiles + first)


def early_kernel(raw, dense, rows, acc_ref):
    depth = raw.shape[0]
    acc_ref[...] = dot(rows[:, :depth], raw[...]) + dot(
        rows[:, depth : depth + dense.shape[0]], dense[...]
    )


def encode(values, out):
    width = values.shape[1]
    across = width // LANES
    high = out.shape[1]
    groups = width // GROUP
    lane = lax.broadcasted_iota(jnp.int32, (high, LANES), 1)
    exps = jnp.zeros((high, LANES), jnp.int32)
    for i in range(BLK // high):
        for g in range(groups):
            part = values[i * high : (i + 1) * high, g * GROUP : (g + 1) * GROUP]
            top = jnp.max(jnp.abs(part), axis=1, keepdims=True)
            exp = jnp.maximum(jnp.ceil(jnp.log2(jnp.maximum(top, 2.0**LOW_EXP))), LOW_EXP)
            scaled = jnp.clip(jnp.round(part * jnp.exp2(15.0 - exp)), -32767.0, 32767.0)
            coded = scaled.astype(jnp.int32).astype(jnp.int16)
            for k in range(GROUP // LANES):
                at = i * across + g * (GROUP // LANES) + k
                out[at] = coded[:, k * LANES : (k + 1) * LANES]
            exps = jnp.where(lane == i * groups + g, exp.astype(jnp.int32), exps)
    for n in range(BLK // high * across, out.shape[0]):
        out[n] = exps.astype(jnp.int16)


def cross_kernel(
    tiles, first, place_ref, y_ref, z_dense, rows, acc, coded, y_dense, place, y, sems
):
    copies = fetch([(place_ref, place), (y_ref, y)], sems)
    depth = z_dense.shape[0]
    at = rows.shape[1] - 2 * depth
    total = acc[...] + dot(rows[:, at : at + depth], z_dense[...])
    for copy in copies:
        copy.wait()
    spread(place, y, y_dense, (lax.axis_index("wide") ^ 3) * tiles + first)
    encode(total + dot(rows[:, at + depth :], y_dense[...]), coded)


def finish(rows, z_dense, y_dense):
    depth = z_dense.shape[0]
    at = rows.shape[1] - 2 * depth
    return dot(rows[:, at : at + depth], z_dense[...]) + dot(rows[:, at + depth :], y_dense[...])


def same_kernel(z_dense, y_dense, rows, acc, coded):
    here = slice(2 * BLK, 3 * BLK)
    encode(acc[here] + finish(rows[here], z_dense, y_dense), coded)


def own_kernel(z_dense, y_dense, rows, acc, _, keep_ref, upper_ref, lower_ref):
    here = slice(0, 2 * BLK)
    total = acc[here] + finish(rows[here], z_dense, y_dense)
    keep_ref[...] = total[:BLK]
    upper_ref[...] = total[BLK : BLK + BLK // 2]
    lower_ref[...] = total[BLK + BLK // 2 :]


def join_kernel(flip, coded, *rest):
    bases, (out_ref, whole, sems) = rest[:-3], rest[-3:]
    bases = bases[-2:] if flip else bases[-1:]
    pair = lax.axis_index("pair") ^ flip
    width = whole.shape[1]
    across, groups, high = width // LANES, width // GROUP, coded.shape[1]
    cols = pl.ds(pl.multiple_of(pair * width, LANES), width)
    exps = coded[BLK // high * across].astype(jnp.int32).astype(jnp.float32)
    copies = []
    for i in range(BLK // high):
        base = bases[i * high // bases[0].shape[0]]
        at = i * high % bases[0].shape[0]
        for g in range(groups):
            n = i * groups + g
            scale = jnp.exp2(exps[:, n : n + 1] - 15.0)
            for k in range(GROUP // LANES):
                s = g * (GROUP // LANES) + k
                here = slice(s * LANES, (s + 1) * LANES)
                value = coded[i * across + s].astype(jnp.int32).astype(jnp.float32) * scale
                whole[i * high : (i + 1) * high, here] = base[at : at + high, here] + value
        here = pl.ds(i * high, high)
        copies.append(pltpu.make_async_copy(whole.at[here], out_ref.at[here, cols], sems.at[i]))
        copies[-1].start()
    for copy in copies:
        copy.wait()


def call(kernel, out, operands, places, scratch=(), room=32, **options):
    specs = {"s": SMEM, "v": VMEM, "a": pl.BlockSpec(memory_space=pl.ANY)}
    return pl.pallas_call(
        kernel,
        out_shape=out,
        in_specs=[specs[p] for p in places],
        scratch_shapes=list(scratch),
        compiler_params=pltpu.CompilerParams(vmem_limit_bytes=room * MIB),
        cost_estimate=pl.CostEstimate(flops=1, bytes_accessed=1, transcendentals=0),
        **{"out_specs": jax.tree.map(lambda _: VMEM, out), **options},
    )(*operands)


def swap_body(amplitudes, integrals, tile_list, slab_order, block_list):
    wide_count, pair_count = lax.axis_size("wide"), lax.axis_size("pair")
    depth, width = integrals.shape
    tiles, group = depth // BLK, width // BLK
    keep = block_list.shape[2]
    bf16, f32, i16, i32 = jnp.bfloat16, jnp.float32, jnp.int16, jnp.int32
    sds = jax.ShapeDtypeStruct
    bind = functools.partial

    def move(x, flip_wide, flip_pair=0):
        if flip_wide and flip_pair:
            n = wide_count * pair_count
            flip = flip_wide * pair_count + flip_pair
            return lax.ppermute(x, ("wide", "pair"), [(i, i ^ flip) for i in range(n)])
        if flip_wide:
            return lax.ppermute(x, "wide", [(i, i ^ flip_wide) for i in range(wide_count)])
        return lax.ppermute(x, "pair", [(i, i ^ flip_pair) for i in range(pair_count)])

    lists = block_list.transpose(2, 1, 0)

    head = SPLIT
    tail = tiles - head

    def pack(start, count):
        return call(
            bind(pack_kernel, start),
            sds((count * BLK, keep * BLK), bf16),
            (lists, integrals),
            "aa",
            [
                pltpu.SMEM(lists.shape, i32),
                pltpu.VMEM((count * BLK, width), bf16),
                pltpu.SemaphoreType.DMA((count + 1,)),
            ],
            ROOM,
        )

    cols = amplitudes.shape[1] // 2
    own, far = call(
        bind(mask_kernel, tiles, head),
        (sds((BLK, cols), bf16),) * 2,
        (tile_list, slab_order, amplitudes),
        "aaa",
        [
            pltpu.SMEM(tile_list.shape, i32),
            pltpu.SMEM(slab_order.shape, i32),
            pltpu.VMEM(amplitudes.shape, bf16),
            pltpu.SMEM((2 * cols // BLK,), i32),
            pltpu.SemaphoreType.DMA((3,)),
        ],
        ROOM,
    )
    z_first = move(pack(0, head), 2)
    z_second = move(pack(head, tail), 2)
    far_same = move(far, 4)
    near = move(integrals, 1)
    own_cross = move(own, 0, 1)
    far_cross = move(far_same, 0, 1)

    my_lists = lax.dynamic_index_in_dim(block_list, lax.axis_index("pair"), 1, keepdims=False)
    hit = my_lists[:, :, None] == jnp.arange(group, dtype=i32)[None, None, :]
    order = jnp.arange(1, keep + 1, dtype=i32)[None, :, None]
    place = (jnp.sum(jnp.where(hit, order, 0), axis=1) - 1).reshape(-1)

    raw = call(raw_kernel, sds((2 * depth, width), bf16), (place, integrals, near), "svv")
    y_first = [move(z_first[a : a + PIECE], 1) for a in range(0, head * BLK, PIECE)]
    y_first[0], own_cross = lax.optimization_barrier((y_first[0], own_cross))
    dense_first = call(
        bind(first_kernel, tiles),
        sds((2 * head * BLK, width), bf16),
        (place, z_first, *y_first),
        "sv" + "v" * len(y_first),
    )

    def begin(rows):
        return call(early_kernel, sds((rows.shape[0], width), f32), (raw, dense_first, rows), "vvv")

    rows = jnp.concatenate((own, own_cross, far_same), axis=0)
    acc = begin(rows)
    far_cross, acc = lax.optimization_barrier((far_cross, acc))
    cross_acc = begin(far_cross)
    z_second, cross_acc = lax.optimization_barrier((z_second, cross_acc))
    y_second = move(z_second, 1)
    z_dense = call(
        bind(second_kernel, tiles, head),
        sds((tail * BLK, width), bf16),
        (place, z_second),
        "sv",
    )
    coded = BLK * width // (16 * LANES) + 1
    part = sds((BLK // 2, width), f32)
    cross, y_dense = call(
        bind(cross_kernel, tiles, head),
        (sds((coded + 1, 16, LANES), i16), sds((tail * BLK, width), bf16)),
        (place, y_second, z_dense, far_cross, cross_acc),
        "aavvv",
        [
            pltpu.SMEM(place.shape, i32),
            pltpu.VMEM(y_second.shape, bf16),
            pltpu.SemaphoreType.DMA((2,)),
        ],
    )
    got_cross = move(cross, 4, 1)
    same = call(
        same_kernel, sds((coded, 16, LANES), i16), (z_dense, y_dense, rows, acc), "vvvv"
    )
    got_same = move(same, 4)
    keep_rows, upper, lower = call(
        own_kernel,
        (sds((BLK, width), f32), part, part),
        (z_dense, y_dense, rows, acc, same),
        "vvvva",
    )

    def join(flip, coded, *bases):
        return call(
            bind(join_kernel, flip),
            sds((BLK, pair_count * width), f32),
            (coded, *bases),
            "v" + ("vv" if flip else "av"),
            [pltpu.VMEM((BLK, width), f32), pltpu.SemaphoreType.DMA((BLK // 16,))],
            out_specs=pl.BlockSpec(memory_space=pltpu.HBM),
            input_output_aliases={} if flip else {1: 0},
        )

    half_done = join(1, got_cross, move(upper, 0, 1), move(lower, 0, 1))
    return join(0, got_same, half_done, keep_rows)


def solution(mesh):
    placed = (
        P(("grp", "wide", "pair"), None),
        P(("grp", "wide"), "pair"),
        P("grp", None),
        P("grp"),
        P("grp", None, None),
    )
    swapped = mesh.shape["wide"] == 8 and mesh.shape["pair"] == 2
    return jax.shard_map(
        swap_body if swapped else gather_body,
        mesh=mesh,
        in_specs=placed,
        out_specs=P(("grp", "wide", "pair"), None),
        check_vma=False,
    )
```

```python
import functools

import jax
import jax.numpy as jnp
from jax import lax
from jax.experimental import pallas as pl
from jax.experimental.pallas import tpu as pltpu
from jax.sharding import PartitionSpec as P

BLK = 64
LANES = 128
GROUP = 256
LOW_EXP = -100.0
ROOM = 60
PIECE = 192
SPLIT = 3
VMEM = pl.BlockSpec(memory_space=pltpu.VMEM)
SMEM = pl.BlockSpec(memory_space=pltpu.SMEM)
MIB = 1024 * 1024


def gather_body(amplitudes, integrals, tile_list, slab_order, block_list):
    rows_dev, virt_cols = amplitudes.shape
    virt_tiles = virt_cols // BLK
    own_count = rows_dev // BLK
    pair_count = lax.axis_size("pair")
    group_count = own_count * pair_count
    wide_index = lax.axis_index("wide")
    pair_index = lax.axis_index("pair")
    slab_ids = lax.dynamic_slice_in_dim(slab_order, wide_index * group_count, group_count)
    own_ids = lax.dynamic_slice_in_dim(slab_ids, pair_index * own_count, own_count)
    own_lists = jnp.take(tile_list, own_ids, axis=0)
    tiles_four = amplitudes.reshape(own_count, BLK, virt_tiles, BLK)
    tile_ids = jnp.arange(virt_tiles, dtype=jnp.int32)
    present = jnp.any(own_lists[:, :, None] == tile_ids[None, None, :], axis=1).astype(
        amplitudes.dtype
    )
    masked = (tiles_four * present[:, None, :, None]).reshape(rows_dev, virt_cols)
    slab_rows = lax.all_gather(masked, "pair", axis=0, tiled=True)
    group_tiles = integrals.shape[1] // BLK
    my_lists = lax.dynamic_index_in_dim(block_list, pair_index, 1, keepdims=False)
    group_ids = jnp.arange(group_tiles, dtype=jnp.int32)
    live = jnp.any(my_lists[:, :, None] == group_ids[None, None, :], axis=1).astype(integrals.dtype)
    shard_block = lax.all_gather(integrals, "wide", axis=0, tiled=True)
    qtiles = shard_block.shape[0] // BLK
    masked_block = shard_block.reshape(qtiles, BLK, group_tiles, BLK) * live[:, None, :, None]
    masked_block = masked_block.reshape(shard_block.shape)
    ladder_slab = jnp.dot(slab_rows, masked_block, preferred_element_type=jnp.float32)
    return lax.all_to_all(ladder_slab, "pair", split_axis=0, concat_axis=1, tiled=True)


def low_lanes(rows):
    return lax.broadcasted_iota(jnp.int32, (rows, LANES), 1) < BLK


def half(index):
    return pl.ds(pl.multiple_of((index // 2) * LANES, LANES), LANES)


def fetch(pairs, sems):
    copies = [pltpu.make_async_copy(s, d, sems.at[n]) for n, (s, d) in enumerate(pairs)]
    for copy in copies:
        copy.start()
    return copies


def pack_kernel(start, lists_ref, block_ref, out, lists, block, sems):
    wide, pair = lax.axis_index("wide"), lax.axis_index("pair")
    tiles = block_ref.shape[0] // BLK
    keep = out.shape[1] // BLK
    count = out.shape[0] // BLK
    rows = [pl.ds(i * BLK, BLK) for i in range(count)]
    sources = [block_ref.at[pl.ds((start + i) * BLK, BLK)] for i in range(count)]
    copies = fetch(
        [(lists_ref, lists)] + [(s, block.at[r]) for s, r in zip(sources, rows)], sems
    )
    copies[0].wait()
    low = low_lanes(BLK)
    for i in range(count):
        copies[1 + i].wait()
        u = wide * tiles + start + i
        for j in range(keep // 2):
            even, odd = lists[2 * j, pair, u], lists[2 * j + 1, pair, u]
            left = pltpu.roll(block[rows[i], half(even)], (even % 2) * BLK, 1)
            right = pltpu.roll(block[rows[i], half(odd)], BLK - (odd % 2) * BLK, 1)
            out[rows[i], j * LANES : (j + 1) * LANES] = jnp.where(low, left, right)


def raw_kernel(place, own_ref, near_ref, dense):
    wide = lax.axis_index("wide")
    depth, width = own_ref.shape
    tiles, group = depth // BLK, width // BLK
    low = low_lanes(BLK)
    for block, source in ((own_ref, wide), (near_ref, wide ^ 1)):
        for i in range(tiles):
            base = (source * tiles + i) * group
            here = pl.ds(pl.multiple_of((source % 2) * depth + i * BLK, BLK), BLK)
            for s in range(group // 2):
                cols = slice(s * LANES, (s + 1) * LANES)
                flag = jnp.where(low, place[base + 2 * s], place[base + 2 * s + 1])
                dense[here, cols] = jnp.where(flag >= 0, block[i * BLK : (i + 1) * BLK, cols], 0)


def spread(place, packed, dense, source_row):
    tiles = packed.shape[0] // BLK
    group = dense.shape[1] // BLK
    low = low_lanes(BLK)
    for i in range(tiles):
        here = slice(i * BLK, (i + 1) * BLK)
        base = (source_row + i) * group
        for s in range(group // 2):
            even, odd = place[base + 2 * s], place[base + 2 * s + 1]
            left_at, right_at = jnp.maximum(even, 0), jnp.maximum(odd, 0)
            left = pltpu.roll(packed[here, half(left_at)], (left_at % 2) * BLK, 1)
            right = pltpu.roll(packed[here, half(right_at)], BLK - (right_at % 2) * BLK, 1)
            flag = jnp.where(low, even, odd)
            dense[here, s * LANES : (s + 1) * LANES] = jnp.where(
                flag >= 0, jnp.where(low, left, right), 0
            )


def mask_kernel(
    tiles, head, tile_ref, slab_ref, amp_ref, own, far, tile_list, slab, amp, present, sems
):
    wide, pair = lax.axis_index("wide"), lax.axis_index("pair")
    copies = fetch([(tile_ref, tile_list), (slab_ref, slab), (amp_ref, amp)], sems)
    count = amp_ref.shape[1] // BLK
    for t in range(count):
        present[t] = 0
    copies[0].wait()
    copies[1].wait()
    tile = slab[wide * 2 + pair]
    for k in range(tile_list.shape[1]):
        present[tile_list[tile, k]] = 1
    chip = ((wide // 2) % 2) * 2 * tiles
    order = [chip + t for t in range(2 * tiles)]
    for first, last in ((0, head), (head, tiles)):
        for source in (wide ^ 2, wide ^ 3):
            order += [(source % 4) * tiles + t for t in range(first, last)]
    low = low_lanes(BLK)
    copies[2].wait()
    for side, out in ((1 - wide // 4, far), (wide // 4, own)):
        base = side * (count // 2)
        for b in range(count // 4):
            even, odd = base + order[2 * b], base + order[2 * b + 1]
            left = pltpu.roll(amp[:, half(even)], (even % 2) * BLK, 1)
            right = pltpu.roll(amp[:, half(odd)], BLK - (odd % 2) * BLK, 1)
            flag = jnp.where(low, present[even], present[odd])
            out[:, b * LANES : (b + 1) * LANES] = jnp.where(
                flag > 0, jnp.where(low, left, right), 0
            )


def dot(a, b):
    return jnp.dot(a, b, preferred_element_type=jnp.float32)


def first_kernel(tiles, place, z_ref, *rest):
    wide = lax.axis_index("wide")
    y_refs, dense = rest[:-1], rest[-1]
    row = 0
    for blocks, source in (((z_ref,), wide ^ 2), (y_refs, wide ^ 3)):
        tile = source * tiles
        for block in blocks:
            size = block.shape[0]
            spread(place, block, dense.at[row : row + size], tile)
            row, tile = row + size, tile + size // BLK


def second_kernel(tiles, first, place, z_ref, dense):
    spread(place, z_ref, dense, (lax.axis_index("wide") ^ 2) * tiles + first)


def early_kernel(raw, dense, rows, acc_ref):
    depth = raw.shape[0]
    acc_ref[...] = dot(rows[:, :depth], raw[...]) + dot(
        rows[:, depth : depth + dense.shape[0]], dense[...]
    )


def encode(values, out):
    width = values.shape[1]
    across = width // LANES
    high = out.shape[1]
    groups = width // GROUP
    lane = lax.broadcasted_iota(jnp.int32, (high, LANES), 1)
    exps = jnp.zeros((high, LANES), jnp.int32)
    for i in range(BLK // high):
        for g in range(groups):
            part = values[i * high : (i + 1) * high, g * GROUP : (g + 1) * GROUP]
            top = jnp.max(jnp.abs(part), axis=1, keepdims=True)
            exp = jnp.maximum(jnp.ceil(jnp.log2(jnp.maximum(top, 2.0**LOW_EXP))), LOW_EXP)
            scaled = jnp.clip(jnp.round(part * jnp.exp2(15.0 - exp)), -32767.0, 32767.0)
            coded = scaled.astype(jnp.int32).astype(jnp.int16)
            for k in range(GROUP // LANES):
                at = i * across + g * (GROUP // LANES) + k
                out[at] = coded[:, k * LANES : (k + 1) * LANES]
            exps = jnp.where(lane == i * groups + g, exp.astype(jnp.int32), exps)
    for n in range(BLK // high * across, out.shape[0]):
        out[n] = exps.astype(jnp.int16)


def cross_kernel(tiles, first, place_ref, y_ref, z_dense, rows, acc, coded, y_dense, place, sems):
    copies = fetch([(place_ref, place)], sems)
    depth = z_dense.shape[0]
    at = rows.shape[1] - 2 * depth
    here = slice(rows.shape[0] - BLK, rows.shape[0])
    total = acc[here] + dot(rows[here, at : at + depth], z_dense[...])
    copies[0].wait()
    spread(place, y_ref, y_dense, (lax.axis_index("wide") ^ 3) * tiles + first)
    encode(total + dot(rows[here, at + depth :], y_dense[...]), coded)


def finish(rows, z_dense, y_dense):
    depth = z_dense.shape[0]
    at = rows.shape[1] - 2 * depth
    return dot(rows[:, at : at + depth], z_dense[...]) + dot(rows[:, at + depth :], y_dense[...])


def same_kernel(z_dense, y_dense, rows, acc, coded):
    here = slice(rows.shape[0] - BLK, rows.shape[0])
    encode(acc[here] + finish(rows[here], z_dense, y_dense), coded)


def own_kernel(z_dense, y_dense, rows, acc, _, keep_ref, upper_ref, lower_ref):
    here = slice(0, 2 * BLK)
    total = acc[here] + finish(rows[here], z_dense, y_dense)
    keep_ref[...] = total[:BLK]
    upper_ref[...] = total[BLK : BLK + BLK // 2]
    lower_ref[...] = total[BLK + BLK // 2 :]


def join_kernel(flip, coded, *rest):
    bases, (out_ref, whole, sems) = rest[:-3], rest[-3:]
    bases = bases[-2:] if flip else bases[-1:]
    pair = lax.axis_index("pair") ^ flip
    width = whole.shape[1]
    across, groups, high = width // LANES, width // GROUP, coded.shape[1]
    cols = pl.ds(pl.multiple_of(pair * width, LANES), width)
    exps = coded[BLK // high * across].astype(jnp.int32).astype(jnp.float32)
    copies = []
    for i in range(BLK // high):
        base = bases[i * high // bases[0].shape[0]]
        at = i * high % bases[0].shape[0]
        for g in range(groups):
            n = i * groups + g
            scale = jnp.exp2(exps[:, n : n + 1] - 15.0)
            for k in range(GROUP // LANES):
                s = g * (GROUP // LANES) + k
                here = slice(s * LANES, (s + 1) * LANES)
                value = coded[i * across + s].astype(jnp.int32).astype(jnp.float32) * scale
                whole[i * high : (i + 1) * high, here] = base[at : at + high, here] + value
        here = pl.ds(i * high, high)
        copies.append(pltpu.make_async_copy(whole.at[here], out_ref.at[here, cols], sems.at[i]))
        copies[-1].start()
    for copy in copies:
        copy.wait()


def call(kernel, out, operands, places, scratch=(), room=32, **options):
    specs = {"s": SMEM, "v": VMEM, "a": pl.BlockSpec(memory_space=pl.ANY)}
    return pl.pallas_call(
        kernel,
        out_shape=out,
        in_specs=[specs[p] for p in places],
        scratch_shapes=list(scratch),
        compiler_params=pltpu.CompilerParams(vmem_limit_bytes=room * MIB),
        cost_estimate=pl.CostEstimate(flops=1, bytes_accessed=1, transcendentals=0),
        **{"out_specs": jax.tree.map(lambda _: VMEM, out), **options},
    )(*operands)


def swap_body(amplitudes, integrals, tile_list, slab_order, block_list):
    wide_count, pair_count = lax.axis_size("wide"), lax.axis_size("pair")
    depth, width = integrals.shape
    tiles, group = depth // BLK, width // BLK
    keep = block_list.shape[2]
    bf16, f32, i16, i32 = jnp.bfloat16, jnp.float32, jnp.int16, jnp.int32
    sds = jax.ShapeDtypeStruct
    bind = functools.partial

    def move(x, flip_wide, flip_pair=0):
        if flip_wide and flip_pair:
            n = wide_count * pair_count
            flip = flip_wide * pair_count + flip_pair
            return lax.ppermute(x, ("wide", "pair"), [(i, i ^ flip) for i in range(n)])
        if flip_wide:
            return lax.ppermute(x, "wide", [(i, i ^ flip_wide) for i in range(wide_count)])
        return lax.ppermute(x, "pair", [(i, i ^ flip_pair) for i in range(pair_count)])

    lists = block_list.transpose(2, 1, 0)

    head = SPLIT
    tail = tiles - head

    def pack(start, count):
        return call(
            bind(pack_kernel, start),
            sds((count * BLK, keep * BLK), bf16),
            (lists, integrals),
            "aa",
            [
                pltpu.SMEM(lists.shape, i32),
                pltpu.VMEM((count * BLK, width), bf16),
                pltpu.SemaphoreType.DMA((count + 1,)),
            ],
            ROOM,
        )

    cols = amplitudes.shape[1] // 2
    own, far = call(
        bind(mask_kernel, tiles, head),
        (sds((BLK, cols), bf16),) * 2,
        (tile_list, slab_order, amplitudes),
        "aaa",
        [
            pltpu.SMEM(tile_list.shape, i32),
            pltpu.SMEM(slab_order.shape, i32),
            pltpu.VMEM(amplitudes.shape, bf16),
            pltpu.SMEM((2 * cols // BLK,), i32),
            pltpu.SemaphoreType.DMA((3,)),
        ],
        ROOM,
    )
    z_first = move(pack(0, head), 2)
    z_second = move(pack(head, tail), 2)
    far_same = move(far, 4)
    near = move(integrals, 1)
    own_cross = move(own, 0, 1)
    far_cross = move(far_same, 0, 1)

    my_lists = lax.dynamic_index_in_dim(block_list, lax.axis_index("pair"), 1, keepdims=False)
    hit = my_lists[:, :, None] == jnp.arange(group, dtype=i32)[None, None, :]
    order = jnp.arange(1, keep + 1, dtype=i32)[None, :, None]
    place = (jnp.sum(jnp.where(hit, order, 0), axis=1) - 1).reshape(-1)

    raw = call(raw_kernel, sds((2 * depth, width), bf16), (place, integrals, near), "svv")
    y_first = [move(z_first[a : a + PIECE], 1) for a in range(0, head * BLK, PIECE)]
    y_first[0], own_cross = lax.optimization_barrier((y_first[0], own_cross))
    dense_first = call(
        bind(first_kernel, tiles),
        sds((2 * head * BLK, width), bf16),
        (place, z_first, *y_first),
        "sv" + "v" * len(y_first),
    )

    def begin(rows):
        return call(early_kernel, sds((rows.shape[0], width), f32), (raw, dense_first, rows), "vvv")

    rows = jnp.concatenate((own, own_cross, far_same), axis=0)
    acc = begin(rows)
    far_cross, acc = lax.optimization_barrier((far_cross, acc))
    z_second, far_cross = lax.optimization_barrier((z_second, far_cross))
    y_second = move(z_second, 1)
    cross_acc = begin(far_cross)
    z_dense = call(
        bind(second_kernel, tiles, head),
        sds((tail * BLK, width), bf16),
        (place, z_second),
        "sv",
    )
    coded = BLK * width // (16 * LANES) + 1
    part = sds((BLK // 2, width), f32)
    same, y_dense = call(
        bind(cross_kernel, tiles, head),
        (sds((coded + 1, 16, LANES), i16), sds((tail * BLK, width), bf16)),
        (place, y_second, z_dense, rows, acc),
        "avvvv",
        [pltpu.SMEM(place.shape, i32), pltpu.SemaphoreType.DMA((1,))],
    )
    got_same = move(same, 4)
    cross = call(
        same_kernel, sds((coded, 16, LANES), i16), (z_dense, y_dense, far_cross, cross_acc), "vvvv"
    )
    got_cross = move(cross, 4, 1)
    keep_rows, upper, lower = call(
        own_kernel,
        (sds((BLK, width), f32), part, part),
        (z_dense, y_dense, rows, acc, cross),
        "vvvva",
    )

    def join(flip, coded, *bases):
        return call(
            bind(join_kernel, flip),
            sds((BLK, pair_count * width), f32),
            (coded, *bases),
            "v" + ("avv" if flip else "v"),
            [pltpu.VMEM((BLK, width), f32), pltpu.SemaphoreType.DMA((BLK // 16,))],
            out_specs=pl.BlockSpec(memory_space=pltpu.HBM),
            input_output_aliases={1: 0} if flip else {},
        )

    half_done = join(0, got_same, keep_rows)
    return join(1, got_cross, half_done, move(upper, 0, 1), move(lower, 0, 1))


def solution(mesh):
    placed = (
        P(("grp", "wide", "pair"), None),
        P(("grp", "wide"), "pair"),
        P("grp", None),
        P("grp"),
        P("grp", None, None),
    )
    swapped = mesh.shape["wide"] == 8 and mesh.shape["pair"] == 2
    return jax.shard_map(
        swap_body if swapped else gather_body,
        mesh=mesh,
        in_specs=placed,
        out_specs=P(("grp", "wide", "pair"), None),
        check_vma=False,
    )
```

```python
import functools

import jax
import jax.numpy as jnp
from jax import lax
from jax.experimental import pallas as pl
from jax.experimental.pallas import tpu as pltpu
from jax.sharding import PartitionSpec as P

BLK = 64
LANES = 128
GROUP = 256
LOW_EXP = -100.0
ROOM = 60
PIECE = 192
SPLIT = 3
VMEM = pl.BlockSpec(memory_space=pltpu.VMEM)
SMEM = pl.BlockSpec(memory_space=pltpu.SMEM)
MIB = 1024 * 1024


def gather_body(amplitudes, integrals, tile_list, slab_order, block_list):
    rows_dev, virt_cols = amplitudes.shape
    virt_tiles = virt_cols // BLK
    own_count = rows_dev // BLK
    pair_count = lax.axis_size("pair")
    group_count = own_count * pair_count
    wide_index = lax.axis_index("wide")
    pair_index = lax.axis_index("pair")
    slab_ids = lax.dynamic_slice_in_dim(slab_order, wide_index * group_count, group_count)
    own_ids = lax.dynamic_slice_in_dim(slab_ids, pair_index * own_count, own_count)
    own_lists = jnp.take(tile_list, own_ids, axis=0)
    tiles_four = amplitudes.reshape(own_count, BLK, virt_tiles, BLK)
    tile_ids = jnp.arange(virt_tiles, dtype=jnp.int32)
    present = jnp.any(own_lists[:, :, None] == tile_ids[None, None, :], axis=1).astype(
        amplitudes.dtype
    )
    masked = (tiles_four * present[:, None, :, None]).reshape(rows_dev, virt_cols)
    slab_rows = lax.all_gather(masked, "pair", axis=0, tiled=True)
    group_tiles = integrals.shape[1] // BLK
    my_lists = lax.dynamic_index_in_dim(block_list, pair_index, 1, keepdims=False)
    group_ids = jnp.arange(group_tiles, dtype=jnp.int32)
    live = jnp.any(my_lists[:, :, None] == group_ids[None, None, :], axis=1).astype(integrals.dtype)
    shard_block = lax.all_gather(integrals, "wide", axis=0, tiled=True)
    qtiles = shard_block.shape[0] // BLK
    masked_block = shard_block.reshape(qtiles, BLK, group_tiles, BLK) * live[:, None, :, None]
    masked_block = masked_block.reshape(shard_block.shape)
    ladder_slab = jnp.dot(slab_rows, masked_block, preferred_element_type=jnp.float32)
    return lax.all_to_all(ladder_slab, "pair", split_axis=0, concat_axis=1, tiled=True)


def low_lanes(rows):
    return lax.broadcasted_iota(jnp.int32, (rows, LANES), 1) < BLK


def half(index):
    return pl.ds(pl.multiple_of((index // 2) * LANES, LANES), LANES)


def fetch(pairs, sems):
    copies = [pltpu.make_async_copy(s, d, sems.at[n]) for n, (s, d) in enumerate(pairs)]
    for copy in copies:
        copy.start()
    return copies


def pack_kernel(start, lists_ref, block_ref, out, lists, block, sems):
    wide, pair = lax.axis_index("wide"), lax.axis_index("pair")
    tiles = block_ref.shape[0] // BLK
    keep = out.shape[1] // BLK
    count = out.shape[0] // BLK
    rows = [pl.ds(i * BLK, BLK) for i in range(count)]
    sources = [block_ref.at[pl.ds((start + i) * BLK, BLK)] for i in range(count)]
    copies = fetch(
        [(lists_ref, lists)] + [(s, block.at[r]) for s, r in zip(sources, rows)], sems
    )
    copies[0].wait()
    low = low_lanes(BLK)
    for i in range(count):
        copies[1 + i].wait()
        u = wide * tiles + start + i
        for j in range(keep // 2):
            even, odd = lists[2 * j, pair, u], lists[2 * j + 1, pair, u]
            left = pltpu.roll(block[rows[i], half(even)], (even % 2) * BLK, 1)
            right = pltpu.roll(block[rows[i], half(odd)], BLK - (odd % 2) * BLK, 1)
            out[rows[i], j * LANES : (j + 1) * LANES] = jnp.where(low, left, right)


def raw_kernel(place, own_ref, near_ref, dense):
    wide = lax.axis_index("wide")
    depth, width = own_ref.shape
    tiles, group = depth // BLK, width // BLK
    low = low_lanes(BLK)
    for block, source in ((own_ref, wide), (near_ref, wide ^ 1)):
        for i in range(tiles):
            base = (source * tiles + i) * group
            here = pl.ds(pl.multiple_of((source % 2) * depth + i * BLK, BLK), BLK)
            for s in range(group // 2):
                cols = slice(s * LANES, (s + 1) * LANES)
                flag = jnp.where(low, place[base + 2 * s], place[base + 2 * s + 1])
                dense[here, cols] = jnp.where(flag >= 0, block[i * BLK : (i + 1) * BLK, cols], 0)


def spread(place, packed, dense, source_row):
    tiles = packed.shape[0] // BLK
    group = dense.shape[1] // BLK
    low = low_lanes(BLK)
    for i in range(tiles):
        here = slice(i * BLK, (i + 1) * BLK)
        base = (source_row + i) * group
        for s in range(group // 2):
            even, odd = place[base + 2 * s], place[base + 2 * s + 1]
            left_at, right_at = jnp.maximum(even, 0), jnp.maximum(odd, 0)
            left = pltpu.roll(packed[here, half(left_at)], (left_at % 2) * BLK, 1)
            right = pltpu.roll(packed[here, half(right_at)], BLK - (right_at % 2) * BLK, 1)
            flag = jnp.where(low, even, odd)
            dense[here, s * LANES : (s + 1) * LANES] = jnp.where(
                flag >= 0, jnp.where(low, left, right), 0
            )


def mask_kernel(
    tiles, head, tile_ref, slab_ref, amp_ref, own, far, tile_list, slab, amp, present, sems
):
    wide, pair = lax.axis_index("wide"), lax.axis_index("pair")
    copies = fetch([(tile_ref, tile_list), (slab_ref, slab), (amp_ref, amp)], sems)
    count = amp_ref.shape[1] // BLK
    for t in range(count):
        present[t] = 0
    copies[0].wait()
    copies[1].wait()
    tile = slab[wide * 2 + pair]
    for k in range(tile_list.shape[1]):
        present[tile_list[tile, k]] = 1
    chip = ((wide // 2) % 2) * 2 * tiles
    order = [chip + t for t in range(2 * tiles)]
    for first, last in ((0, head), (head, tiles)):
        for source in (wide ^ 2, wide ^ 3):
            order += [(source % 4) * tiles + t for t in range(first, last)]
    low = low_lanes(BLK)
    copies[2].wait()
    for side, out in ((1 - wide // 4, far), (wide // 4, own)):
        base = side * (count // 2)
        for b in range(count // 4):
            even, odd = base + order[2 * b], base + order[2 * b + 1]
            left = pltpu.roll(amp[:, half(even)], (even % 2) * BLK, 1)
            right = pltpu.roll(amp[:, half(odd)], BLK - (odd % 2) * BLK, 1)
            flag = jnp.where(low, present[even], present[odd])
            out[:, b * LANES : (b + 1) * LANES] = jnp.where(
                flag > 0, jnp.where(low, left, right), 0
            )


def dot(a, b):
    return jnp.dot(a, b, preferred_element_type=jnp.float32)


def first_kernel(tiles, place, z_ref, *rest):
    wide = lax.axis_index("wide")
    y_refs, dense = rest[:-1], rest[-1]
    row = 0
    for blocks, source in (((z_ref,), wide ^ 2), (y_refs, wide ^ 3)):
        tile = source * tiles
        for block in blocks:
            size = block.shape[0]
            spread(place, block, dense.at[row : row + size], tile)
            row, tile = row + size, tile + size // BLK


def second_kernel(tiles, first, place, z_ref, dense):
    spread(place, z_ref, dense, (lax.axis_index("wide") ^ 2) * tiles + first)


def early_kernel(raw, dense, rows, acc_ref):
    depth = raw.shape[0]
    acc_ref[...] = dot(rows[:, :depth], raw[...]) + dot(
        rows[:, depth : depth + dense.shape[0]], dense[...]
    )


def encode(values, out):
    width = values.shape[1]
    across = width // LANES
    high = out.shape[1]
    groups = width // GROUP
    lane = lax.broadcasted_iota(jnp.int32, (high, LANES), 1)
    exps = jnp.zeros((high, LANES), jnp.int32)
    for i in range(BLK // high):
        for g in range(groups):
            part = values[i * high : (i + 1) * high, g * GROUP : (g + 1) * GROUP]
            top = jnp.max(jnp.abs(part), axis=1, keepdims=True)
            exp = jnp.maximum(jnp.ceil(jnp.log2(jnp.maximum(top, 2.0**LOW_EXP))), LOW_EXP)
            scaled = jnp.clip(jnp.round(part * jnp.exp2(15.0 - exp)), -32767.0, 32767.0)
            coded = scaled.astype(jnp.int32).astype(jnp.int16)
            for k in range(GROUP // LANES):
                at = i * across + g * (GROUP // LANES) + k
                out[at] = coded[:, k * LANES : (k + 1) * LANES]
            exps = jnp.where(lane == i * groups + g, exp.astype(jnp.int32), exps)
    for n in range(BLK // high * across, out.shape[0]):
        out[n] = exps.astype(jnp.int16)


def cross_kernel(tiles, first, place_ref, y_ref, z_dense, rows, acc, coded, y_dense, place, sems):
    copies = fetch([(place_ref, place)], sems)
    depth = z_dense.shape[0]
    at = rows.shape[1] - 2 * depth
    here = slice(rows.shape[0] - BLK, rows.shape[0])
    total = acc[here] + dot(rows[here, at : at + depth], z_dense[...])
    copies[0].wait()
    spread(place, y_ref, y_dense, (lax.axis_index("wide") ^ 3) * tiles + first)
    encode(total + dot(rows[here, at + depth :], y_dense[...]), coded)


def finish(rows, z_dense, y_dense):
    depth = z_dense.shape[0]
    at = rows.shape[1] - 2 * depth
    return dot(rows[:, at : at + depth], z_dense[...]) + dot(rows[:, at + depth :], y_dense[...])


def same_kernel(z_dense, y_dense, rows, acc, coded):
    here = slice(rows.shape[0] - BLK, rows.shape[0])
    encode(acc[here] + finish(rows[here], z_dense, y_dense), coded)


def own_kernel(z_dense, y_dense, rows, acc, _, keep_ref, upper_ref, lower_ref):
    here = slice(0, 2 * BLK)
    total = acc[here] + finish(rows[here], z_dense, y_dense)
    keep_ref[...] = total[:BLK]
    upper_ref[...] = total[BLK : BLK + BLK // 2]
    lower_ref[...] = total[BLK + BLK // 2 :]


def join_kernel(flip, coded, *rest):
    bases, (out_ref, whole, sems) = rest[:-3], rest[-3:]
    bases = bases[-2:] if flip else bases[-1:]
    pair = lax.axis_index("pair") ^ flip
    width = whole.shape[1]
    across, groups, high = width // LANES, width // GROUP, coded.shape[1]
    cols = pl.ds(pl.multiple_of(pair * width, LANES), width)
    exps = coded[BLK // high * across].astype(jnp.int32).astype(jnp.float32)
    copies = []
    for i in range(BLK // high):
        base = bases[i * high // bases[0].shape[0]]
        at = i * high % bases[0].shape[0]
        for g in range(groups):
            n = i * groups + g
            scale = jnp.exp2(exps[:, n : n + 1] - 15.0)
            for k in range(GROUP // LANES):
                s = g * (GROUP // LANES) + k
                here = slice(s * LANES, (s + 1) * LANES)
                value = coded[i * across + s].astype(jnp.int32).astype(jnp.float32) * scale
                whole[i * high : (i + 1) * high, here] = base[at : at + high, here] + value
        here = pl.ds(i * high, high)
        copies.append(pltpu.make_async_copy(whole.at[here], out_ref.at[here, cols], sems.at[i]))
        copies[-1].start()
    for copy in copies:
        copy.wait()


def call(kernel, out, operands, places, scratch=(), room=32, **options):
    specs = {"s": SMEM, "v": VMEM, "a": pl.BlockSpec(memory_space=pl.ANY)}
    return pl.pallas_call(
        kernel,
        out_shape=out,
        in_specs=[specs[p] for p in places],
        scratch_shapes=list(scratch),
        compiler_params=pltpu.CompilerParams(vmem_limit_bytes=room * MIB),
        cost_estimate=pl.CostEstimate(flops=1, bytes_accessed=1, transcendentals=0),
        **{"out_specs": jax.tree.map(lambda _: VMEM, out), **options},
    )(*operands)


def swap_body(amplitudes, integrals, tile_list, slab_order, block_list):
    wide_count, pair_count = lax.axis_size("wide"), lax.axis_size("pair")
    depth, width = integrals.shape
    tiles, group = depth // BLK, width // BLK
    keep = block_list.shape[2]
    bf16, f32, i16, i32 = jnp.bfloat16, jnp.float32, jnp.int16, jnp.int32
    sds = jax.ShapeDtypeStruct
    bind = functools.partial

    def move(x, flip_wide, flip_pair=0):
        if flip_wide and flip_pair:
            n = wide_count * pair_count
            flip = flip_wide * pair_count + flip_pair
            return lax.ppermute(x, ("wide", "pair"), [(i, i ^ flip) for i in range(n)])
        if flip_wide:
            return lax.ppermute(x, "wide", [(i, i ^ flip_wide) for i in range(wide_count)])
        return lax.ppermute(x, "pair", [(i, i ^ flip_pair) for i in range(pair_count)])

    lists = block_list.transpose(2, 1, 0)

    head = SPLIT
    tail = tiles - head

    def pack(start, count):
        return call(
            bind(pack_kernel, start),
            sds((count * BLK, keep * BLK), bf16),
            (lists, integrals),
            "aa",
            [
                pltpu.SMEM(lists.shape, i32),
                pltpu.VMEM((count * BLK, width), bf16),
                pltpu.SemaphoreType.DMA((count + 1,)),
            ],
            ROOM,
        )

    cols = amplitudes.shape[1] // 2
    own, far = call(
        bind(mask_kernel, tiles, head),
        (sds((BLK, cols), bf16),) * 2,
        (tile_list, slab_order, amplitudes),
        "aaa",
        [
            pltpu.SMEM(tile_list.shape, i32),
            pltpu.SMEM(slab_order.shape, i32),
            pltpu.VMEM(amplitudes.shape, bf16),
            pltpu.SMEM((2 * cols // BLK,), i32),
            pltpu.SemaphoreType.DMA((3,)),
        ],
        ROOM,
    )
    z_first = move(pack(0, head), 2)
    z_second = move(pack(head, tail), 2)
    far_same = move(far, 4)
    near = move(integrals, 1)
    own_cross = move(own, 0, 1)
    far_cross = move(far_same, 0, 1)

    my_lists = lax.dynamic_index_in_dim(block_list, lax.axis_index("pair"), 1, keepdims=False)
    hit = my_lists[:, :, None] == jnp.arange(group, dtype=i32)[None, None, :]
    order = jnp.arange(1, keep + 1, dtype=i32)[None, :, None]
    place = (jnp.sum(jnp.where(hit, order, 0), axis=1) - 1).reshape(-1)

    raw = call(raw_kernel, sds((2 * depth, width), bf16), (place, integrals, near), "svv")
    y_first = [move(z_first[a : a + PIECE], 1) for a in range(0, head * BLK, PIECE)]
    y_first[0], own_cross = lax.optimization_barrier((y_first[0], own_cross))
    dense_first = call(
        bind(first_kernel, tiles),
        sds((2 * head * BLK, width), bf16),
        (place, z_first, *y_first),
        "sv" + "v" * len(y_first),
    )

    def begin(rows):
        return call(early_kernel, sds((rows.shape[0], width), f32), (raw, dense_first, rows), "vvv")

    rows = jnp.concatenate((own, own_cross, far_same), axis=0)
    acc = begin(rows)
    far_cross, acc = lax.optimization_barrier((far_cross, acc))
    z_second, far_cross = lax.optimization_barrier((z_second, far_cross))
    y_second = move(z_second, 1)
    cross_acc = begin(far_cross)
    z_dense = call(
        bind(second_kernel, tiles, head),
        sds((tail * BLK, width), bf16),
        (place, z_second),
        "sv",
    )
    coded = BLK * width // (16 * LANES) + 1
    part = sds((BLK // 2, width), f32)
    same, y_dense = call(
        bind(cross_kernel, tiles, head),
        (sds((coded, 16, LANES), i16), sds((tail * BLK, width), bf16)),
        (place, y_second, z_dense, rows, acc),
        "avvvv",
        [pltpu.SMEM(place.shape, i32), pltpu.SemaphoreType.DMA((1,))],
    )
    got_same = move(same, 4)
    cross = call(
        same_kernel, sds((coded, 16, LANES), i16), (z_dense, y_dense, far_cross, cross_acc), "vvvv"
    )
    got_cross = move(cross, 4, 1)
    keep_rows, upper, lower = call(
        own_kernel,
        (sds((BLK, width), f32), part, part),
        (z_dense, y_dense, rows, acc, cross),
        "vvvva",
    )

    def join(flip, coded, *bases):
        return call(
            bind(join_kernel, flip),
            sds((BLK, pair_count * width), f32),
            (coded, *bases),
            "v" + ("avv" if flip else "v"),
            [pltpu.VMEM((BLK, width), f32), pltpu.SemaphoreType.DMA((BLK // 16,))],
            out_specs=pl.BlockSpec(memory_space=pltpu.HBM),
            input_output_aliases={1: 0} if flip else {},
        )

    half_done = join(0, got_same, keep_rows)
    return join(1, got_cross, half_done, move(upper, 0, 1), move(lower, 0, 1))


def solution(mesh):
    placed = (
        P(("grp", "wide", "pair"), None),
        P(("grp", "wide"), "pair"),
        P("grp", None),
        P("grp"),
        P("grp", None, None),
    )
    swapped = mesh.shape["wide"] == 8 and mesh.shape["pair"] == 2
    return jax.shard_map(
        swap_body if swapped else gather_body,
        mesh=mesh,
        in_specs=placed,
        out_specs=P(("grp", "wide", "pair"), None),
        check_vma=False,
    )
```
